128 devices in a mesh: section: 2 (over core), expert: 2 (over x_lo), dp: 32 (over z, y, x_hi).
Axes of the slice: x: 4 (x_hi: 2, x_lo: 2; x = x_hi * 2 + x_lo), y: 4, z: 4, core: 2. Of those that a mesh axis runs over, the one named last changes fastest.
Arguments:
- inputs: bfloat16 [2, 256, 2048], P(None, ('section', 'expert')), may hold values from -6 to 6
- cotangent: bfloat16 [2, 256, 2048], P(None, ('section', 'expert')), may hold values from -6 to 6
- w_gate: bfloat16 [8, 7168, 2048], P('expert', 'dp', 'section'), may hold values from -0.125 to 0.125
- w_up: bfloat16 [8, 7168, 2048], P('expert', 'dp', 'section'), may hold values from -0.125 to 0.125
- w_down: bfloat16 [8, 7168, 2048], P('expert', 'dp', 'section'), may hold values from -0.0625 to 0.0625
- router: float32 [2048, 8], replicated, may hold values from -0.25 to 0.25
- norm_gain: float32 [2048], replicated, may hold values from 0.5 to 1.5
- routes: int32 [2, 256, 2], P(None, ('section', 'expert')), may hold values from 0 to 7, all different within a row; in each aligned block of 64 rows (0 to 63, 64 to 127, ..., all dimensions but the last counted through in order) at most 32 rows name the same one
Outputs:
- layer_out: bfloat16 [2, 256, 2048], P(None, ('section', 'expert'))
- grad_inputs: bfloat16 [2, 256, 2048], P(None, ('section', 'expert'))
- grad_router: float32 [2048, 8], replicated
- grad_gain: float32 [2048], replicated
The draws below stay inside these ranges and needn't reach their ends.
Inputs may be any that keep to these rules, and one draw needn't show every extreme that they name: `routes`: the two experts of a token differ. In every micro-batch and every aligned block of 64 tokens (the tokens of one index of section and expert), no expert is named by more than 32 tokens, a bound that some block reaches.
All inputs are finite; a program needn't handle non-finite values.
Results may differ from the reference program's by a relative error of at most 0.0073.
Values may be sent and summed in bfloat16 or wider, within the bound.
No kernel may reach another device: no remote copies, remote signals or barrier semaphores. Data moves between devices by JAX's collectives and lax.ppermute only.
A program may use at most 128 MiB of HBM per device.

```python
import math
import jax
import jax.numpy as jnp
import numpy as np
from jax import lax

D = 2048
FF = 7168
MICRO = 2
TOK_MB = 64
EXPERTS = 8
TOKENS = 256
CAP = 32
N_DP = 32


def block_scale(own_key, extent, shards, least, high):
    def one(dim, parts):
        steps = jax.random.uniform(jax.random.fold_in(jax.random.fold_in(own_key, 6), dim), (parts,), jnp.float32, least / len(shards), high / len(shards))
        return jnp.repeat(jnp.exp(steps), extent[dim] // parts).reshape((-1,) + (1,) * (len(extent) - dim - 1))

    factor_of = one(*shards[0])
    for cut in shards[1:]:
        factor_of = factor_of * one(*cut)
    return factor_of


def routed_block(rng, own, number, rows, amount, top, most, lean):
    ranking = jax.random.permutation(rng, amount)
    crowded, common = portions_of(amount, rows * top, most, lean, True), portions_of(amount, rows * top, most, lean, False)
    places = jnp.arange(amount)

    def named(tallies, turn):
        used = int((tallies > 0).sum())
        fixed = max(1, used // 4)
        shifted = fixed + (places - fixed + turn * (used - fixed)) % max(1, amount - fixed)
        return jnp.zeros((amount,), jnp.int32).at[ranking[jnp.where(places < fixed, places, shifted)]].set(jnp.asarray(tallies, jnp.int32))

    tallies = jnp.where(number % 4 == 0, named(crowded, number // 4), named(common, number - number // 4 - 1))
    mixed = jax.random.permutation(jax.random.fold_in(own, 3), amount)
    donor, receiver = mixed[0:amount // 2 * 2:2], mixed[1:amount // 2 * 2:2]
    slack = jnp.minimum(tallies[donor] - 1, most - tallies[receiver]) // 2
    slack = jnp.where((donor == ranking[0]) | (receiver == ranking[0]) | (tallies[receiver] == 0), 0, jnp.maximum(slack, 0))
    shifted = jax.random.randint(jax.random.fold_in(own, 4), (amount // 2,), 0, 1 << 20) % (slack + 1)
    tallies = tallies.at[donor].add(-shifted).at[receiver].add(shifted)
    members = jnp.searchsorted(jnp.cumsum(tallies), jnp.arange(rows * top), side="right").astype(jnp.int32)
    grid = members.reshape(top, rows).T
    grid = grid[jax.random.permutation(jax.random.fold_in(own, 1), rows)]
    turn = jax.random.randint(jax.random.fold_in(own, 2), (rows, 1), 0, top)
    return jnp.take_along_axis(grid, (jnp.arange(top)[None, :] + turn) % top, axis=1)


def portions_of(count, total, limit, skew, full):
    portions = [(1 << 20) // math.isqrt(grade ** skew) + 1 for grade in range(1, count + 1)]
    largest = limit if full else min(limit, max(-(-total // count), total * portions[0] // sum(portions)))
    least = 1 if total - largest >= count - 1 else 0
    holding, rest = [largest] + [least] * (count - 1), total - largest - least * (count - 1)
    while rest > 0:
        candidates = [i for i in range(1, count) if holding[i] < largest] or [i for i in range(1, count) if holding[i] < limit]
        pool, budget = sum([portions[i] for i in candidates]), rest
        for i in candidates:
            addition = min(limit - holding[i], max(1, budget * portions[i] // pool), rest)
            holding[i] = holding[i] + addition
            rest = rest - addition
    return np.array(holding)


def noise(own_key, extent, width, limit, shards=(), held_as=jnp.bfloat16):
    gain = block_scale(own_key, extent, shards, -0.22, 0.18) if shards else 1.0
    values = jax.random.normal(own_key, extent, jnp.float32) * width * gain
    return jnp.minimum(jnp.maximum(values, -limit), limit).astype(held_as)


def setup_inputs(seed: int = 0) -> dict:
    arg_keys = jax.random.split(jax.random.key(seed), 9)
    inputs = noise(arg_keys[0], (MICRO, TOKENS, D), 1.0, 6.0, ((1, 4),))
    cotangent = noise(arg_keys[1], (MICRO, TOKENS, D), 1.0, 6.0, ((1, 4),))
    w_gate = noise(arg_keys[2], (EXPERTS, FF, D), D ** -0.5, 0.125, ((0, 2), (1, 32), (2, 2)))
    w_up = noise(arg_keys[3], (EXPERTS, FF, D), D ** -0.5, 0.125, ((0, 2), (1, 32), (2, 2)))
    w_down = noise(arg_keys[4], (EXPERTS, FF, D), FF ** -0.5, 0.0625, ((0, 2), (1, 32), (2, 2)))
    router = noise(arg_keys[5], (D, EXPERTS), (D // 4) ** -0.5, 0.25, (), jnp.float32)
    norm_gain = jnp.clip(1.0 + 0.1 * jax.random.normal(arg_keys[6], (D,), jnp.float32), 0.5, 1.5)
    routes_keys = jax.random.split(jax.random.fold_in(arg_keys[7], 1), MICRO * TOKENS // TOK_MB)
    routes_turns = jax.random.permutation(jax.random.fold_in(arg_keys[7], 3), MICRO * TOKENS // TOK_MB)
    routes = jax.vmap(lambda own, number: routed_block(jax.random.fold_in(arg_keys[7], 2), own, number, TOK_MB, EXPERTS, 2, CAP, 2))(routes_keys, routes_turns).reshape((MICRO, TOKENS, 2))
    return {"inputs": inputs, "cotangent": cotangent, "w_gate": w_gate, "w_up": w_up, "w_down": w_down, "router": router, "norm_gain": norm_gain, "routes": routes}


EPSILON = 1e-05

def normalize(wide_in, gain_row, router_map):
    scaling = lax.rsqrt(lax.optimization_barrier(jnp.mean(wide_in * wide_in, axis=-1, keepdims=True)) + EPSILON)
    normed = wide_in * scaling * gain_row
    logits = jnp.dot(normed, router_map, precision=lax.Precision.HIGHEST, preferred_element_type=jnp.float32)
    return (normed, logits)

def gate_pair(logits, expert_ids):
    chosen = jnp.take_along_axis(logits, expert_ids, axis=1)
    leading = jax.nn.sigmoid(chosen[:, 0] - chosen[:, 1])
    return (leading, 1.0 - leading)

def block_terms(rows_e, back_e, gate_blocks, up_blocks, down_blocks):

    def advance(carry, maps):
        part_sum, drow_sum = carry
        gate_map, up_map, down_map = maps
        pre_gate = jnp.dot(rows_e, gate_map.T, preferred_element_type=jnp.float32)
        pre_up = jnp.dot(rows_e, up_map.T, preferred_element_type=jnp.float32)
        squash = jax.nn.sigmoid(pre_gate)
        hidden = (pre_gate * squash * pre_up).astype(jnp.bfloat16)
        block_out = jnp.dot(hidden, down_map, preferred_element_type=jnp.float32).astype(jnp.bfloat16)
        hidden_grad = jnp.dot(back_e, down_map.T, preferred_element_type=jnp.float32)
        gate_grad = (hidden_grad * pre_up * (squash + pre_gate * squash * (1.0 - squash))).astype(jnp.bfloat16)
        up_grad = (hidden_grad * pre_gate * squash).astype(jnp.bfloat16)
        row_grad = (jnp.dot(gate_grad, gate_map, preferred_element_type=jnp.float32) + jnp.dot(up_grad, up_map, preferred_element_type=jnp.float32)).astype(jnp.bfloat16)
        return ((part_sum + block_out.astype(jnp.float32), drow_sum + row_grad.astype(jnp.float32)), None)
    zero_rows = jnp.zeros((rows_e.shape[0], D), jnp.float32)
    (part_sum, drow_sum), unused = lax.scan(advance, (zero_rows, zero_rows), (gate_blocks, up_blocks, down_blocks))
    return (part_sum, drow_sum)

def expert_slots(named_mask, groups):
    blocks = named_mask.astype(jnp.int32).reshape(groups, TOK_MB)
    rank_in = (jnp.cumsum(blocks, axis=1) - blocks).astype(jnp.int32)
    base_slot = (jnp.arange(groups, dtype=jnp.int32) * CAP)[:, None]
    slot_idx = jnp.where(blocks > 0, base_slot + rank_in, groups * CAP)
    return slot_idx.reshape(-1).astype(jnp.int32)

def reference(inputs, cotangent, w_gate, w_up, w_down, router, norm_gain, routes):
    groups = TOKENS // TOK_MB
    block_width = FF // N_DP
    layer_list, grad_list = ([], [])
    gain_total = jnp.zeros((D,), jnp.float32)
    router_total = jnp.zeros((D, EXPERTS), jnp.float32)
    for micro_idx in range(MICRO):
        expert_ids = routes[micro_idx]
        wide_in = inputs[micro_idx].astype(jnp.float32)
        wide_up = cotangent[micro_idx].astype(jnp.float32)
        (normed, logits), pullback = jax.vjp(normalize, wide_in, norm_gain, router)
        rows_low = normed.astype(jnp.bfloat16)
        leading, trailing = gate_pair(logits, expert_ids)
        back_first = (leading[:, None] * wide_up).astype(jnp.bfloat16)
        back_second = (trailing[:, None] * wide_up).astype(jnp.bfloat16)
        mixed = jnp.zeros((TOKENS, D), jnp.float32)
        dnormed = jnp.zeros((TOKENS, D), jnp.float32)
        first_dg = jnp.zeros((TOKENS,), jnp.float32)
        second_dg = jnp.zeros((TOKENS,), jnp.float32)
        for expert in range(EXPERTS):
            on_first = expert_ids[:, 0] == expert
            on_second = expert_ids[:, 1] == expert
            named_mask = on_first | on_second
            slot_idx = expert_slots(named_mask, groups)
            slot_safe = jnp.minimum(slot_idx, groups * CAP - 1).astype(jnp.int32)
            rows_e = jnp.zeros((groups * CAP, D), jnp.bfloat16).at[slot_idx].set(rows_low, mode='drop')
            back_tok = jnp.where(on_first[:, None], back_first, jnp.where(on_second[:, None], back_second, jnp.zeros_like(back_first)))
            back_e = jnp.zeros((groups * CAP, D), jnp.bfloat16).at[slot_idx].set(back_tok, mode='drop')
            weight = jnp.where(on_first, leading, jnp.where(on_second, trailing, jnp.zeros_like(leading)))
            gate_blocks = w_gate[expert].reshape(N_DP, block_width, D)
            up_blocks = w_up[expert].reshape(N_DP, block_width, D)
            down_blocks = w_down[expert].reshape(N_DP, block_width, D)
            part_sum, drow_sum = block_terms(rows_e, back_e, gate_blocks, up_blocks, down_blocks)
            taken_rows = jnp.where(named_mask[:, None], jnp.take(part_sum, slot_safe, axis=0), 0.0)
            mixed = mixed + weight[:, None] * taken_rows
            dnormed = dnormed + jnp.where(named_mask[:, None], jnp.take(drow_sum, slot_safe, axis=0), 0.0)
            inner_sum = lax.optimization_barrier(jnp.sum(wide_up * taken_rows, axis=1))
            first_dg = first_dg + jnp.where(on_first, inner_sum, 0.0)
            second_dg = second_dg + jnp.where(on_second, inner_sum, 0.0)
        layer_list.append((wide_in + mixed).astype(jnp.bfloat16))
        delta_gate = leading * trailing * (first_dg - second_dg)
        columns = jnp.arange(EXPERTS, dtype=jnp.int32)[None, :]
        dlogits = delta_gate[:, None] * ((expert_ids[:, 0:1] == columns).astype(jnp.float32) - (expert_ids[:, 1:2] == columns).astype(jnp.float32))
        input_grad, gain_grad, router_grad = pullback((dnormed, dlogits))
        grad_list.append((wide_up + input_grad).astype(jnp.bfloat16))
        gain_total = gain_total + gain_grad
        router_total = router_total + router_grad
    return (jnp.stack(layer_list), jnp.stack(grad_list), router_total, gain_total)
```

```python
import functools

import jax
import jax.numpy as jnp
from jax import lax
from jax.experimental import pallas as pl
from jax.experimental.pallas import tpu as pltpu
from jax.sharding import PartitionSpec as P

EPSILON = 1e-05
EXT = 128
F32 = jnp.float32
BF16 = jnp.bfloat16
HIGHEST = lax.Precision.HIGHEST
NT = (((1,), (1,)), ((), ()))
VMEM_BYTES = 40 * 1024 * 1024


def params():
    return pltpu.CompilerParams(vmem_limit_bytes=VMEM_BYTES)


def lanes(rows):
    return lax.broadcasted_iota(jnp.int32, (rows, EXT), 1)


def split_low(value):
    high = value.astype(BF16).astype(F32)
    return high, value - high


def inverse_rms(wide):
    return lax.rsqrt(jnp.mean(wide * wide, axis=-1, keepdims=True) + EPSILON)


def prologue_kernel(x_ref, gain_ref, router_ref, routes_ref, rows_ref, coef_ref):
    width = x_ref.shape[1]
    count = router_ref.shape[0]
    wide = x_ref[...].astype(F32)
    normed = wide * inverse_rms(wide) * gain_ref[...]
    rows_ref[:, :width] = normed.astype(BF16)
    logits = lax.dot_general(normed, router_ref[...], NT, precision=HIGHEST, preferred_element_type=F32)
    first, second = routes_ref[:, 0:1], routes_ref[:, 1:2]
    column = lax.broadcasted_iota(jnp.int32, logits.shape, 1)
    signs = (column == first).astype(F32) - (column == second).astype(F32)
    leading = jax.nn.sigmoid(jnp.sum(signs * logits, axis=1, keepdims=True))
    trailing = 1.0 - leading
    lead_high, lead_low = split_low(leading)
    trail_high, trail_low = split_low(trailing)
    lane = lanes(x_ref.shape[0])

    def place(start, at_first, at_second):
        return jnp.where(lane == first + start, at_first, 0.0) + jnp.where(
            lane == second + start, at_second, 0.0
        )

    extra = (
        place(0, lead_high, trail_high)
        + place(count, lead_low, trail_low)
        + place(2 * count, 1.0, -1.0)
    )
    rows_ref[:, width:] = extra.astype(BF16)
    slope = leading * trailing
    coef_ref[...] = place(0, slope, -slope)


def forward_kernel(
    count,
    meta,
    rows_own, rows_a, rows_b, cot_own, cot_a, cot_b,
    gate_0, gate_1, up_0, up_1, down_0, down_1,
    mix_own, mix_a, mix_b, dgate_ref, dup_ref, sums_ref,
    r_0, r_1, c_0, c_1, acc_0, acc_1, aux,
):
    step = pl.program_id(0)
    local = pl.num_programs(0)
    half = acc_0.shape[1]
    own, sub = rows_own.shape[0], rows_a.shape[0]
    at_0 = pl.multiple_of(meta[0] * half, half)
    at_1 = pl.multiple_of((1 - meta[0]) * half, half)
    parts = ((0, own, rows_own, cot_own), (own, sub, rows_a, cot_a), (own + sub, sub, rows_b, cot_b))

    @pl.when(step == 0)
    def _():
        for start, size, rows, cot in parts:
            r_0[start:start + size, :] = rows[:, pl.ds(at_0, half)]
            r_1[start:start + size, :] = rows[:, pl.ds(at_1, half)]
            c_0[start:start + size, :] = cot[:, pl.ds(at_0, half)]
            c_1[start:start + size, :] = cot[:, pl.ds(at_1, half)]
            aux[start:start + size, :] = rows[:, 2 * half:].astype(F32)
        acc_0[...] = jnp.zeros_like(acc_0)
        acc_1[...] = jnp.zeros_like(acc_1)
        sums_ref[...] = jnp.zeros_like(sums_ref)

    def both(left_0, left_1, map_0, map_1):
        return lax.dot_general(left_0[...], map_0[0], NT, preferred_element_type=F32) + lax.dot_general(
            left_1[...], map_1[0], NT, preferred_element_type=F32
        )

    expert = meta[1] * local + step
    lane = lanes(aux.shape[0])
    extra = aux[...]
    weight = jnp.sum(
        jnp.where((lane == expert) | (lane == expert + count), extra, 0.0), axis=1, keepdims=True
    )
    sign = jnp.sum(jnp.where(lane == expert + 2 * count, extra, 0.0), axis=1, keepdims=True)
    pre_gate = both(r_0, r_1, gate_0, gate_1)
    pre_up = both(r_0, r_1, up_0, up_1)
    dhid = both(c_0, c_1, down_0, down_1)
    squash = jax.nn.sigmoid(pre_gate)
    act = pre_gate * squash
    hidden = act * pre_up
    gate_sum = jnp.sum(hidden * dhid, axis=1, keepdims=True) * sign
    sums_ref[...] += jnp.where(lane == 0, gate_sum, 0.0)
    dhid = dhid * weight
    dgate_ref[0] = (dhid * pre_up * (squash + act * (1.0 - squash))).astype(BF16)
    dup_ref[0] = (dhid * act).astype(BF16)
    weighted = (hidden * weight).astype(BF16)
    acc_0[...] += jnp.dot(weighted, down_0[0], preferred_element_type=F32)
    acc_1[...] += jnp.dot(weighted, down_1[0], preferred_element_type=F32)

    @pl.when(step == local - 1)
    def _():
        for start, size, out in ((0, own, mix_own), (own, sub, mix_a), (own + sub, sub, mix_b)):
            out[:, pl.ds(at_0, half)] = acc_0[start:start + size, :].astype(BF16)
            out[:, pl.ds(at_1, half)] = acc_1[start:start + size, :].astype(BF16)


def backward_kernel(
    meta,
    dgate_ref, dup_ref, gate_0, gate_1, up_0, up_1, rows_own, rows_a, rows_b, sums_ref,
    dn_own, dn_a, dn_b, gain_ext,
    acc_0, acc_1, line, block,
):
    step = pl.program_id(0)
    half = acc_0.shape[1]
    own, sub = rows_own.shape[0], rows_a.shape[0]
    at_0 = pl.multiple_of(meta[0] * half, half)
    at_1 = pl.multiple_of((1 - meta[0]) * half, half)

    @pl.when(step == 0)
    def _():
        acc_0[...] = jnp.zeros_like(acc_0)
        acc_1[...] = jnp.zeros_like(acc_1)

    dgate, dup = dgate_ref[0], dup_ref[0]
    for acc, gate_map, up_map in ((acc_0, gate_0, up_0), (acc_1, gate_1, up_1)):
        acc[...] += jnp.dot(dgate, gate_map[0], preferred_element_type=F32) + jnp.dot(
            dup, up_map[0], preferred_element_type=F32
        )

    @pl.when(step == pl.num_programs(0) - 1)
    def _():
        high, low = split_low(sums_ref[:, 0:1])
        lane = lanes(sums_ref.shape[0])
        extra = jnp.where(lane == 0, high, jnp.where(lane == 1, low, 0.0)).astype(BF16)
        totals = [0.0, 0.0]
        for start, size, out, rows in (
            (0, own, dn_own, rows_own), (own, sub, dn_a, rows_a), (own + sub, sub, dn_b, rows_b),
        ):
            out[:, 2 * half:] = extra[start:start + size, :]
            for which, (acc, at) in enumerate(((acc_0, at_0), (acc_1, at_1))):
                value = acc[start:start + size, :]
                out[:, pl.ds(at, half)] = value.astype(BF16)
                totals[which] += jnp.sum(
                    value * rows[:, pl.ds(at, half)].astype(F32), axis=0, keepdims=True
                )
        line[:, pl.ds(at_0, half)] = totals[0]
        line[:, pl.ds(at_1, half)] = totals[1]
        block[...] = jnp.zeros_like(block)
        for place in range(2 * half // EXT):
            high, low = split_low(line[:, place * EXT:(place + 1) * EXT])
            block[8 * place:8 * place + 1, :] = high
            block[8 * place + 1:8 * place + 2, :] = low
        gain_ext[...] = block[...].astype(BF16)


def pack_kernel(mix_own, mix_a, mix_b, gain_ext, dn_own, dn_a, dn_b, out_ref):
    own, width = mix_own.shape
    sub = mix_a.shape[0]
    for start, mix, grad in ((0, mix_a, dn_a), (sub, mix_b, dn_b)):
        span = slice(start, start + sub)
        out_ref[span, :width] = (mix_own[span, :].astype(F32) + mix[...].astype(F32)).astype(BF16)
        under = slice(own + start, own + start + sub)
        out_ref[under, :width] = (
            dn_own[span, :width].astype(F32) + grad[:, :width].astype(F32)
        ).astype(BF16)
        both = dn_own[span, width:].astype(F32) + grad[:, width:].astype(F32)
        high, low = split_low(jnp.sum(both, axis=1, keepdims=True))
        lane = lanes(sub)
        out_ref[under, width:] = jnp.where(lane == 0, high, jnp.where(lane == 1, low, 0.0)).astype(BF16)
    out_ref[:own, width:] = gain_ext[...]


def finish_kernel(meta, parts_ref, x_ref, cot_ref, coef_ref, gain_ref, router_ref, out_ref):
    chunks, rows, _ = parts_ref.shape
    width = x_ref.shape[2]
    total = parts_ref[0].astype(F32)
    for source in range(1, chunks):
        total = total + parts_ref[source].astype(F32)
    wide = x_ref[0].astype(F32)
    summed, extra = total[:, :width], total[:, width:]
    lane = lanes(rows)
    row = lax.broadcasted_iota(jnp.int32, (rows, EXT), 0)
    is_first = meta[0] < chunks // 2
    layer = wide + summed
    gain_high, gain_low = split_low(extra[0:1, :] + extra[1:2, :])
    layer_extra = jnp.where(row == 0, gain_high, jnp.where(row == 1, gain_low, 0.0))
    sums = extra[:, 0:1] + extra[:, 1:2]
    sum_high, sum_low = split_low(sums)
    grad_extra = jnp.where(lane == 0, sum_high, jnp.where(lane == 1, sum_low, 0.0))
    dlogits = coef_ref[0] * sums
    dnormed = summed
    for expert in range(router_ref.shape[0]):
        dnormed = dnormed + dlogits[:, expert:expert + 1] * router_ref[expert:expert + 1, :]
    scaling = inverse_rms(wide)
    unit = wide * scaling
    dunit = dnormed * gain_ref[...]
    dx = scaling * (dunit - unit * jnp.mean(dunit * unit, axis=-1, keepdims=True))
    grad = cot_ref[0].astype(F32) + dx
    out = jnp.where(is_first, layer, grad).astype(BF16)
    out_extra = jnp.where(is_first, layer_extra, grad_extra).astype(BF16)
    for place in range(chunks):
        out_ref[place, :, :width] = out
        out_ref[place, :, width:] = out_extra


def tail_kernel(all_ref, x_ref, coef_ref, layer_ref, grad_ref, sums_ref, wide_sums):
    chunks = all_ref.shape[0]
    width = x_ref.shape[1]
    mid = chunks // 2
    layer_ref[...] = all_ref[:mid, :, :width]
    grad_ref[...] = all_ref[mid:, :, :width]
    for place in range(mid):
        wide_sums[8 * place:8 * place + 8, :] = all_ref[mid + place, :, width:].astype(F32)
    dlogits = coef_ref[...] * (wide_sums[:, 0:1] + wide_sums[:, 1:2])
    wide = x_ref[...].astype(F32)
    unit = wide * inverse_rms(wide)
    sums_ref[0:8, :] = jnp.dot(dlogits.T[0:8, :], unit, precision=HIGHEST, preferred_element_type=F32)
    sums_ref[8:16, :] = jnp.zeros((8, width), F32)
    for place in range(mid):
        extra = all_ref[place, :, width:].astype(F32)
        sums_ref[8:9, place * EXT:(place + 1) * EXT] = extra[0:1, :] + extra[1:2, :]


def whole(array):
    return pl.BlockSpec(array.shape, lambda *_: (0,) * len(array.shape))


def struct(*shape, dtype=BF16):
    return jax.ShapeDtypeStruct(shape, dtype)


def shards(n_dp, inputs, cotangent, w_gate, w_up, w_down, router, norm_gain, routes):
    micro, sub, width = inputs.shape
    own = micro * sub
    total = 2 * own
    local, units, half = w_gate.shape
    count = router.shape[1]
    section, expert = lax.axis_index("section"), lax.axis_index("expert")
    place = lax.axis_index("dp")
    meta = jnp.stack([section, expert]).astype(jnp.int32)

    def around(shift):
        pairs = []
        for e in range(2):
            for d in range(n_dp):
                x = (d % 2 * 2 + e + shift) % 4
                pairs.append((e * n_dp + d, (x % 2) * n_dp + d - d % 2 + x // 2))
        return pairs

    def up_x(array):
        return lax.ppermute(array, ("expert", "dp"), around(1))

    def down_x(array):
        return lax.ppermute(array, ("expert", "dp"), around(3))

    def other_core(array):
        return lax.ppermute(array, "section", [(0, 1), (1, 0)])

    def other_expert(array):
        return lax.ppermute(array, "expert", [(0, 1), (1, 0)])

    maps = [(w, other_core(w)) for w in (w_gate, w_up, w_down)]
    (gate_0, gate_1), (up_0, up_1), (down_0, down_1) = maps
    cot_a, cot_b = up_x(cotangent[0]), down_x(cotangent[1])
    flat_x = inputs.reshape(own, width)
    flat_cot = cotangent.reshape(own, width)
    gain_row = norm_gain.reshape(1, width)
    router_rows = router.T
    rows_own, coef = pl.pallas_call(
        prologue_kernel,
        out_shape=(struct(own, width + EXT), struct(own, EXT, dtype=F32)),
        compiler_params=params(),
    )(flat_x, gain_row, router_rows, routes.reshape(own, 2))
    rows_a, rows_b = up_x(rows_own[:sub]), down_x(rows_own[sub:])

    map_spec = pl.BlockSpec((1, units, half), lambda i, m: (i, 0, 0))
    unit_spec = pl.BlockSpec((1, total, units), lambda i, m: (i, 0, 0))
    token_args = (rows_own, rows_a, rows_b, flat_cot, cot_a, cot_b)
    forward_out = (
        struct(own, width), struct(sub, width), struct(sub, width),
        struct(local, total, units), struct(local, total, units), struct(total, EXT, dtype=F32),
    )
    mix_own, mix_a, mix_b, dgate, dup, sums = pl.pallas_call(
        functools.partial(forward_kernel, count),
        grid_spec=pltpu.PrefetchScalarGridSpec(
            num_scalar_prefetch=1,
            grid=(local,),
            in_specs=[whole(a) for a in token_args] + [map_spec] * 6,
            out_specs=[whole(a) for a in forward_out[:3]] + [unit_spec, unit_spec, whole(forward_out[5])],
            scratch_shapes=[pltpu.VMEM((total, half), BF16)] * 4
            + [pltpu.VMEM((total, half), F32)] * 2
            + [pltpu.VMEM((total, EXT), F32)],
        ),
        out_shape=forward_out,
        compiler_params=params(),
        cost_estimate=pl.CostEstimate(
            flops=16 * total * local * units * half, bytes_accessed=24 * local * units * half, transcendentals=0
        ),
    )(meta, *token_args, gate_0, gate_1, up_0, up_1, down_0, down_1)
    mix_a, mix_b = up_x(mix_a), down_x(mix_b)

    backward_out = (struct(own, width + EXT), struct(sub, width + EXT), struct(sub, width + EXT), struct(own, EXT))
    row_args = (rows_own, rows_a, rows_b, sums)
    dn_own, dn_a, dn_b, gain_ext = pl.pallas_call(
        backward_kernel,
        grid_spec=pltpu.PrefetchScalarGridSpec(
            num_scalar_prefetch=1,
            grid=(local,),
            in_specs=[unit_spec] * 2 + [map_spec] * 4 + [whole(a) for a in row_args],
            out_specs=[whole(a) for a in backward_out],
            scratch_shapes=[pltpu.VMEM((total, half), F32)] * 2
            + [pltpu.VMEM((1, width), F32), pltpu.VMEM((own, EXT), F32)],
        ),
        out_shape=backward_out,
        compiler_params=params(),
        cost_estimate=pl.CostEstimate(
            flops=8 * total * local * units * half, bytes_accessed=16 * local * units * half, transcendentals=0
        ),
    )(meta, dgate, dup, gate_0, gate_1, up_0, up_1, *row_args)
    dn_a, dn_b = up_x(dn_a), down_x(dn_b)

    packed = pl.pallas_call(
        pack_kernel, out_shape=struct(total, width + EXT), compiler_params=params()
    )(mix_own, mix_a, mix_b, gain_ext, dn_own, dn_a, dn_b)
    rows_each = total // n_dp
    chunks = lax.all_to_all(packed.reshape(n_dp, rows_each, width + EXT), "dp", 0, 0, tiled=True)

    blocks = own // rows_each
    spot = jnp.stack([place, place % blocks]).astype(jnp.int32)

    def at_spot(last):
        return pl.BlockSpec((1, rows_each, last), lambda i, m: (m[1], 0, 0))

    finished = pl.pallas_call(
        finish_kernel,
        grid_spec=pltpu.PrefetchScalarGridSpec(
            num_scalar_prefetch=1,
            grid=(1,),
            in_specs=[whole(chunks), at_spot(width), at_spot(width), at_spot(EXT), whole(gain_row), whole(router_rows)],
            out_specs=whole(chunks),
        ),
        out_shape=struct(*chunks.shape),
        compiler_params=params(),
    )(
        spot,
        chunks,
        inputs.reshape(blocks, rows_each, width),
        cotangent.reshape(blocks, rows_each, width),
        coef.reshape(blocks, rows_each, EXT),
        gain_row,
        router_rows,
    )
    gathered = lax.all_to_all(finished, "dp", 0, 0, tiled=True)

    layer, grad, summed = pl.pallas_call(
        tail_kernel,
        out_shape=(
            struct(blocks, rows_each, width), struct(blocks, rows_each, width), struct(16, width, dtype=F32),
        ),
        scratch_shapes=[pltpu.VMEM((own, EXT), F32)],
        compiler_params=params(),
    )(gathered, flat_x, coef)
    summed = summed + other_core(summed)
    summed = summed + other_expert(summed)
    moments = summed[:count]
    grad_router = (moments * gain_row).T
    grad_gain = summed[8] / norm_gain + jnp.sum(router_rows * moments, axis=0)
    return layer.reshape(micro, sub, width), grad.reshape(micro, sub, width), grad_router, grad_gain


def solution(mesh):
    tokens = P(None, ("section", "expert"), None)
    maps = P("expert", "dp", "section")
    return jax.shard_map(
        functools.partial(shards, mesh.shape["dp"]),
        mesh=mesh,
        in_specs=(tokens, tokens, maps, maps, maps, P(), P(), tokens),
        out_specs=(tokens, tokens, P(), P()),
        check_vma=False,
    )
```

```python
import functools

import jax
import jax.numpy as jnp
from jax import lax
from jax.experimental import pallas as pl
from jax.experimental.pallas import tpu as pltpu
from jax.sharding import PartitionSpec as P

EPSILON = 1e-05
EXT = 128
F32 = jnp.float32
BF16 = jnp.bfloat16
HIGHEST = lax.Precision.HIGHEST
NT = (((1,), (1,)), ((), ()))
VMEM_BYTES = 16 * 1024 * 1024
EXPERT_VMEM = 60 * 1024 * 1024
TILE = 256


def params(limit=VMEM_BYTES):
    return pltpu.CompilerParams(vmem_limit_bytes=limit)


def lanes(rows):
    return lax.broadcasted_iota(jnp.int32, (rows, EXT), 1)


def split_low(value):
    high = value.astype(BF16).astype(F32)
    return high, value - high


def inverse_rms(wide):
    return lax.rsqrt(jnp.mean(wide * wide, axis=-1, keepdims=True) + EPSILON)


def prologue_kernel(x_ref, gain_ref, router_ref, routes_ref, rows_ref, extra_ref, coef_ref):
    count = router_ref.shape[0]
    wide = x_ref[...].astype(F32)
    normed = wide * inverse_rms(wide) * gain_ref[...]
    rows_ref[...] = normed.astype(BF16)
    logits = lax.dot_general(normed, router_ref[...], NT, precision=HIGHEST, preferred_element_type=F32)
    first, second = routes_ref[:, 0:1], routes_ref[:, 1:2]
    column = lax.broadcasted_iota(jnp.int32, logits.shape, 1)
    signs = (column == first).astype(F32) - (column == second).astype(F32)
    leading = jax.nn.sigmoid(jnp.sum(signs * logits, axis=1, keepdims=True))
    trailing = 1.0 - leading
    lead_high, lead_low = split_low(leading)
    trail_high, trail_low = split_low(trailing)
    lane = lanes(x_ref.shape[0])

    def place(start, at_first, at_second):
        return jnp.where(lane == first + start, at_first, 0.0) + jnp.where(
            lane == second + start, at_second, 0.0
        )

    extra = (
        place(0, lead_high, trail_high)
        + place(count, lead_low, trail_low)
        + place(2 * count, 1.0, -1.0)
    )
    extra_ref[...] = extra.astype(BF16)
    slope = leading * trailing
    coef_ref[...] = place(0, slope, -slope)


def tiles_of(extent, size):
    return [(start, min(size, extent - start)) for start in range(0, extent, size)]

def expert_kernel(
    count, units, tile, fresh,
    meta, rows_ref, cot_ref, extra_ref, side_ref, gate_0, gate_1, up_0, up_1, down_0, down_1,
    mix_ref, grad_ref, params_ref,
    g_0, g_1, u_0, u_1, d_0, d_1, r_0, r_1, c_0, c_1, hid, dgate, dup, sems,
):
    hidden_units, half = gate_0.shape
    total = rows_ref.shape[0]
    width = 2 * half
    local = hidden_units // units
    at_0 = pl.multiple_of(meta[0] * half, half)
    at_1 = pl.multiple_of((1 - meta[0]) * half, half)
    tiles = tiles_of(hidden_units, tile)
    copies = []
    for number, (start, size) in enumerate(tiles):
        group = []
        for which, (source, target) in enumerate(
            ((gate_0, g_0), (gate_1, g_1), (up_0, u_0), (up_1, u_1), (down_0, d_0), (down_1, d_1))
        ):
            copy = pltpu.make_async_copy(
                source.at[pl.ds(start, size), :], target.at[pl.ds(start, size), :], sems.at[number, which]
            )
            copy.start()
            group.append(copy)
        copies.append(group)

    scaling = inverse_rms(rows_ref[...].astype(F32)) if fresh else None
    for at, r, c in ((at_0, r_0, c_0), (at_1, r_1, c_1)):
        rows = rows_ref[:, pl.ds(at, half)]
        if fresh:
            rows = (rows.astype(F32) * scaling * side_ref[:, pl.ds(at, half)]).astype(BF16)
        r[...] = rows
        c[...] = cot_ref[:, pl.ds(at, half)]

    lane = lanes(total)
    extra = extra_ref[...].astype(F32)
    weights, signs = [], []
    for which in range(local):
        expert = meta[1] * local + which
        weights.append(
            jnp.sum(jnp.where((lane == expert) | (lane == expert + count), extra, 0.0), axis=1, keepdims=True)
        )
        signs.append(jnp.sum(jnp.where(lane == expert + 2 * count, extra, 0.0), axis=1, keepdims=True))

    sums = jnp.zeros((total, 1), F32)
    for group, (start, size) in zip(copies, tiles):
        for copy in group:
            copy.wait()
        span = slice(start, start + size)

        def both(left_0, left_1, map_0, map_1):
            return lax.dot_general(left_0[...], map_0[span, :], NT, preferred_element_type=F32) + lax.dot_general(
                left_1[...], map_1[span, :], NT, preferred_element_type=F32
            )

        pre_gate = both(r_0, r_1, g_0, g_1)
        pre_up = both(r_0, r_1, u_0, u_1)
        dhid = both(c_0, c_1, d_0, d_1)
        column = lax.broadcasted_iota(jnp.int32, (total, size), 1) + start
        first = start // units
        weight, sign = weights[first], signs[first]
        for later in range(first + 1, (start + size - 1) // units + 1):
            weight = jnp.where(column < later * units, weight, weights[later])
            sign = jnp.where(column < later * units, sign, signs[later])
        squash = jax.nn.sigmoid(pre_gate)
        act = pre_gate * squash
        hidden = act * pre_up
        sums = sums + jnp.sum(hidden * dhid * sign, axis=1, keepdims=True)
        dhid = dhid * weight
        dgate[:, span] = (dhid * pre_up * (squash + act * (1.0 - squash))).astype(BF16)
        dup[:, span] = (dhid * act).astype(BF16)
        hid[:, span] = (hidden * weight).astype(BF16)

    high, low = split_low(sums)
    grad_ref[:, width:] = jnp.where(lane == 0, high, jnp.where(lane == 1, low, 0.0)).astype(BF16)
    share = jnp.where(lane < count, extra + pltpu.roll(extra, EXT - count, 1), 0.0)
    dlogits = share * (1.0 - share) * pltpu.roll(extra, EXT - 2 * count, 1) * sums
    high, low = split_low(dlogits)
    sides = jnp.concatenate([high.T[:count], low.T[:count]], axis=0).astype(BF16)
    for at, g, u, d, r in ((at_0, g_0, u_0, d_0, r_0), (at_1, g_1, u_1, d_1, r_1)):
        there = pl.ds(at, half)
        mix_ref[:, there] = jnp.dot(hid[...], d[...], preferred_element_type=F32).astype(BF16)
        grad = jnp.dot(dgate[...], g[...], preferred_element_type=F32) + jnp.dot(
            dup[...], u[...], preferred_element_type=F32
        )
        grad_ref[:, there] = grad.astype(BF16)
        routing = jnp.dot(sides, r[...], preferred_element_type=F32)
        routing = routing[:count] + routing[count:]
        moved = jnp.sum(grad * r[...].astype(F32), axis=0, keepdims=True)
        moved = jnp.broadcast_to(moved, routing.shape)
        if not fresh:
            routing = routing + side_ref[:count, there]
            moved = moved + side_ref[count:, there]
        params_ref[:count, there] = routing
        params_ref[count:, there] = moved


def pack_kernel(mix_own, mix_in, grad_own, grad_in, sums_own, sums_core, sums_across, sums_diagonal, out_ref):
    own, width = mix_own.shape
    out_ref[:own, :width] = (mix_own[...].astype(F32) + mix_in[...].astype(F32)).astype(BF16)
    out_ref[own:, :width] = (grad_own[:, :width].astype(F32) + grad_in[:, :width].astype(F32)).astype(BF16)
    both = grad_own[:, width:].astype(F32) + grad_in[:, width:].astype(F32)
    high, low = split_low(jnp.sum(both, axis=1, keepdims=True))
    lane = lanes(own)
    gate_sums = jnp.where(lane == 0, high, jnp.where(lane == 1, low, 0.0))
    totals = (sums_own[...] + sums_core[...]) + (sums_across[...] + sums_diagonal[...])
    upper, row = lanes(8) >= EXT // 2, lax.broadcasted_iota(jnp.int32, (8, EXT), 0)
    for pair in range(own // 16):
        routing, ends = [], []
        for place in (2 * pair, 2 * pair + 1):
            part = totals[:, place * EXT:(place + 1) * EXT]
            routing.append(part[:8])
            moved = jnp.where(row == 0, part[8:], jnp.where(row == 1, pltpu.roll(part[8:], EXT // 2, 1), 0.0))
            ends.append(jnp.where(upper, moved, gate_sums[8 * place:8 * place + 8]))
        span = slice(16 * pair, 16 * pair + 16)
        out_ref[span, width:] = jnp.concatenate(routing, axis=0).astype(BF16)
        out_ref[own + 16 * pair:own + 16 * pair + 16, width:] = jnp.concatenate(ends, axis=0).astype(BF16)


def finish_kernel(meta, parts_ref, x_ref, cot_ref, coef_ref, gain_ref, router_ref, out_ref):
    chunks = parts_ref.shape[0]
    width = x_ref.shape[2]
    total = parts_ref[0].astype(F32)
    for source in range(1, chunks):
        total = total + parts_ref[source].astype(F32)
    wide = x_ref[0].astype(F32)
    summed, extra = total[:, :width], total[:, width:]
    layer = wide + summed
    dlogits = coef_ref[0] * (extra[:, 0:1] + extra[:, 1:2])
    dnormed = summed
    for expert in range(router_ref.shape[0]):
        dnormed = dnormed + dlogits[:, expert:expert + 1] * router_ref[expert:expert + 1, :]
    scaling = inverse_rms(wide)
    unit = wide * scaling
    dunit = dnormed * gain_ref[...]
    dx = scaling * (dunit - unit * jnp.mean(dunit * unit, axis=-1, keepdims=True))
    grad = cot_ref[0].astype(F32) + dx
    out = jnp.where(meta[0] < chunks // 2, layer, grad).astype(BF16)
    ends = extra.astype(BF16)
    for place in range(chunks):
        out_ref[place, :, :width] = out
        out_ref[place, :, width:] = ends


def tail_kernel(all_ref, gain_ref, router_ref, layer_ref, grad_ref, grad_router_ref, grad_gain_ref):
    mid = all_ref.shape[0] // 2
    count, width = router_ref.shape
    layer_ref[...] = all_ref[:mid, :, :width]
    grad_ref[...] = all_ref[mid:, :, :width]
    upper = lanes(1) >= EXT // 2
    for place in range(mid):
        span = slice(place * EXT, (place + 1) * EXT)
        routing = all_ref[place, :, width:].astype(F32)
        ends = all_ref[mid + place, :, width:].astype(F32)
        moved = jnp.where(upper, ends[0:1], pltpu.roll(ends[1:2], EXT // 2, 1))
        grad_router_ref[:, span] = routing
        shares = jnp.sum(router_ref[:, span] * routing, axis=0, keepdims=True)
        grad_gain_ref[:, span] = (moved + shares) / gain_ref[:, span]


def whole(array):
    return pl.BlockSpec(array.shape, lambda *_: (0,) * len(array.shape))


def struct(*shape, dtype=BF16):
    return jax.ShapeDtypeStruct(shape, dtype)


def shards(n_dp, inputs, cotangent, w_gate, w_up, w_down, router, norm_gain, routes):
    micro, sub, width = inputs.shape
    own = micro * sub
    local, units, half = w_gate.shape
    count = router.shape[1]
    section, expert = lax.axis_index("section"), lax.axis_index("expert")
    place = lax.axis_index("dp")
    meta = jnp.stack([section, expert]).astype(jnp.int32)

    def around(shift):
        pairs = []
        for e in range(2):
            for d in range(n_dp):
                x = (d % 2 * 2 + e + shift) % 4
                pairs.append((e * n_dp + d, (x % 2) * n_dp + d - d % 2 + x // 2))
        return pairs

    def up_x(array):
        return lax.ppermute(array, ("expert", "dp"), around(1))

    def down_x(array):
        return lax.ppermute(array, ("expert", "dp"), around(3))

    def other_core(array):
        return lax.ppermute(array, "section", [(0, 1), (1, 0)])

    flat_x = inputs.reshape(own, width)
    flat_cot = cotangent.reshape(own, width)
    x_other, cot_other = up_x(flat_x), down_x(flat_cot)
    gate_0, up_0, down_0 = (w.reshape(local * units, half) for w in (w_gate, w_up, w_down))
    gate_1 = other_core(gate_0)
    up_1 = other_core(up_0)
    down_late, gate_1 = lax.optimization_barrier((down_0, gate_1))
    down_1 = other_core(down_late)
    maps = (gate_0, gate_1, up_0, up_1, down_0, down_1)
    gain_row = norm_gain.reshape(1, width)
    router_rows = router.T
    rows_own, extra_own, coef = pl.pallas_call(
        prologue_kernel,
        out_shape=(struct(own, width), struct(own, EXT), struct(own, EXT, dtype=F32)),
        compiler_params=params(),
        cost_estimate=pl.CostEstimate(flops=20_000_000_000, bytes_accessed=2**25, transcendentals=0),
    )(flat_x, gain_row, router_rows, routes.reshape(own, 2))
    extra_other = up_x(extra_own)

    hidden_units = local * units
    near = pl.BlockSpec(memory_space=pltpu.VMEM)
    far = pl.BlockSpec(memory_space=pltpu.HBM)
    sums_shape = struct(2 * count, width, dtype=F32)

    def experts(fresh, rows, cot, extra, side):
        return pl.pallas_call(
            functools.partial(expert_kernel, count, units, TILE, fresh),
            in_specs=[pl.BlockSpec(memory_space=pltpu.SMEM)] + [near] * 4 + [far] * 6,
            out_specs=(near, near, near),
            out_shape=(struct(own, width), struct(own, width + EXT), sums_shape),
            scratch_shapes=[pltpu.VMEM((hidden_units, half), BF16)] * 6
            + [pltpu.VMEM((own, half), BF16)] * 4
            + [pltpu.VMEM((own, hidden_units), BF16)] * 3
            + [pltpu.SemaphoreType.DMA((len(tiles_of(hidden_units, TILE)), 6))],
            compiler_params=params(EXPERT_VMEM),
            cost_estimate=pl.CostEstimate(
                flops=24 * own * hidden_units * half, bytes_accessed=12 * hidden_units * half, transcendentals=0
            ),
        )(meta, rows, cot, extra, side, *maps)

    mix_away, grad_away, sums = experts(True, x_other, cot_other, extra_other, gain_row)
    mix_in, grad_in = up_x(mix_away), down_x(grad_away)
    mix_own, grad_own, sums = experts(False, rows_own, flat_cot, extra_own, sums)
    core = other_core(sums)
    across = lax.ppermute(sums, "expert", [(0, 1), (1, 0)])
    diagonal = lax.ppermute(sums, ("section", "expert"), [(0, 3), (1, 2), (2, 1), (3, 0)])
    packed = pl.pallas_call(pack_kernel, out_shape=struct(2 * own, width + EXT), compiler_params=params())(
        mix_own, mix_in, grad_own, grad_in, sums, core, across, diagonal
    )
    rows_each = 2 * own // n_dp
    chunks = lax.all_to_all(packed.reshape(n_dp, rows_each, width + EXT), "dp", 0, 0, tiled=True)

    blocks = own // rows_each
    spot = jnp.stack([place, place % blocks]).astype(jnp.int32)

    def at_spot(last):
        return pl.BlockSpec((1, rows_each, last), lambda i, m: (m[1], 0, 0))

    finished = pl.pallas_call(
        finish_kernel,
        grid_spec=pltpu.PrefetchScalarGridSpec(
            num_scalar_prefetch=1,
            grid=(1,),
            in_specs=[whole(chunks), at_spot(width), at_spot(width), at_spot(EXT), whole(gain_row), whole(router_rows)],
            out_specs=whole(chunks),
        ),
        out_shape=struct(*chunks.shape),
        compiler_params=params(),
    )(
        spot,
        chunks,
        inputs.reshape(blocks, rows_each, width),
        cotangent.reshape(blocks, rows_each, width),
        coef.reshape(blocks, rows_each, EXT),
        gain_row,
        router_rows,
    )
    gathered = lax.all_to_all(finished, "dp", 0, 0, tiled=True)

    layer, grad, grad_router, grad_gain = pl.pallas_call(
        tail_kernel,
        out_shape=(
            struct(blocks, rows_each, width), struct(blocks, rows_each, width),
            struct(count, width, dtype=F32), struct(1, width, dtype=F32),
        ),
        compiler_params=params(),
    )(gathered, gain_row, router_rows)
    return (
        layer.reshape(micro, sub, width), grad.reshape(micro, sub, width), grad_router.T, grad_gain.reshape(width)
    )


def solution(mesh):
    tokens = P(None, ("section", "expert"), None)
    maps = P("expert", "dp", "section")
    return jax.shard_map(
        functools.partial(shards, mesh.shape["dp"]),
        mesh=mesh,
        in_specs=(tokens, tokens, maps, maps, maps, P(), P(), tokens),
        out_specs=(tokens, tokens, P(), P()),
        check_vma=False,
    )
```

```python
import functools

import jax
import jax.numpy as jnp
from jax import lax
from jax.experimental import pallas as pl
from jax.experimental.pallas import tpu as pltpu
from jax.sharding import PartitionSpec as P

EPSILON = 1e-05
EXT = 128
F32 = jnp.float32
BF16 = jnp.bfloat16
HIGHEST = lax.Precision.HIGHEST
NT = (((1,), (1,)), ((), ()))
VMEM_BYTES = 16 * 1024 * 1024
EXPERT_VMEM = 46 * 1024 * 1024
WIDE_VMEM = 60 * 1024 * 1024
TILE = 256
BACK_TILE = 512


def params(limit=VMEM_BYTES):
    return pltpu.CompilerParams(vmem_limit_bytes=limit)


def lanes(rows):
    return lax.broadcasted_iota(jnp.int32, (rows, EXT), 1)


def split_low(value):
    high = value.astype(BF16).astype(F32)
    return high, value - high


def inverse_rms(wide):
    return lax.rsqrt(jnp.mean(wide * wide, axis=-1, keepdims=True) + EPSILON)


def prologue_kernel(x_ref, gain_ref, router_ref, routes_ref, rows_ref, extra_ref, coef_ref):
    count = router_ref.shape[0]
    wide = x_ref[...].astype(F32)
    normed = wide * inverse_rms(wide) * gain_ref[...]
    rows_ref[...] = normed.astype(BF16)
    logits = lax.dot_general(normed, router_ref[...], NT, precision=HIGHEST, preferred_element_type=F32)
    first, second = routes_ref[:, 0:1], routes_ref[:, 1:2]
    column = lax.broadcasted_iota(jnp.int32, logits.shape, 1)
    signs = (column == first).astype(F32) - (column == second).astype(F32)
    leading = jax.nn.sigmoid(jnp.sum(signs * logits, axis=1, keepdims=True))
    trailing = 1.0 - leading
    lead_high, lead_low = split_low(leading)
    trail_high, trail_low = split_low(trailing)
    lane = lanes(x_ref.shape[0])

    def place(start, at_first, at_second):
        return jnp.where(lane == first + start, at_first, 0.0) + jnp.where(
            lane == second + start, at_second, 0.0
        )

    extra = (
        place(0, lead_high, trail_high)
        + place(count, lead_low, trail_low)
        + place(2 * count, 1.0, -1.0)
    )
    extra_ref[...] = extra.astype(BF16)
    slope = leading * trailing
    coef_ref[...] = place(0, slope, -slope)


def tiles_of(extent, size):
    return [(start, min(size, extent - start)) for start in range(0, extent, size)]

def forward_kernel(
    count, units, tile,
    meta, rows_own, x_other, cot_own, cot_other, extra_own, extra_other, gain_ref,
    gate_0, gate_1, up_0, up_1, down_0, down_1,
    mix_own, mix_a, mix_b, dgate, dup, r_0, r_1, routing_ref, ends_ref,
    g_0, g_1, u_0, u_1, d_0, d_1, c_0, c_1, hid, sems,
):
    hidden_units, half = gate_0.shape
    own, sub = rows_own.shape[0], mix_a.shape[0]
    total = 2 * own
    local = hidden_units // units
    at_0 = pl.multiple_of(meta[0] * half, half)
    at_1 = pl.multiple_of((1 - meta[0]) * half, half)
    tiles = tiles_of(hidden_units, tile)

    def fetch(number):
        start, size = tiles[number]
        group = []
        for which, (source, target) in enumerate(
            ((gate_0, g_0), (gate_1, g_1), (up_0, u_0), (up_1, u_1), (down_0, d_0), (down_1, d_1))
        ):
            copy = pltpu.make_async_copy(
                source.at[pl.ds(start, size), :], target.at[pl.ds(start, size), :], sems.at[number, which]
            )
            copy.start()
            group.append(copy)
        return group

    copies = [fetch(0), fetch(1)]
    scaling = inverse_rms(x_other[...].astype(F32))
    for at, r, c in ((at_0, r_0, c_0), (at_1, r_1, c_1)):
        there = pl.ds(at, half)
        r[:own, :] = rows_own[:, there]
        r[own:, :] = (x_other[:, there].astype(F32) * scaling * gain_ref[:, there]).astype(BF16)
        c[:own, :] = cot_own[:, there]
        c[own:, :] = cot_other[:, there]

    lane = lanes(total)
    extra = jnp.concatenate([extra_own[...], extra_other[...]], axis=0).astype(F32)
    weights, signs = [], []
    for which in range(local):
        expert = meta[1] * local + which
        weights.append(
            jnp.sum(jnp.where((lane == expert) | (lane == expert + count), extra, 0.0), axis=1, keepdims=True)
        )
        signs.append(jnp.sum(jnp.where(lane == expert + 2 * count, extra, 0.0), axis=1, keepdims=True))

    sums = jnp.zeros((total, 1), F32)
    for number, (start, size) in enumerate(tiles):
        if number + 2 < len(tiles):
            copies.append(fetch(number + 2))
        for copy in copies[number]:
            copy.wait()
        span = slice(start, start + size)

        def both(left_0, left_1, map_0, map_1):
            return lax.dot_general(left_0[...], map_0[span, :], NT, preferred_element_type=F32) + lax.dot_general(
                left_1[...], map_1[span, :], NT, preferred_element_type=F32
            )

        pre_gate = both(r_0, r_1, g_0, g_1)
        pre_up = both(r_0, r_1, u_0, u_1)
        dhid = both(c_0, c_1, d_0, d_1)
        column = lax.broadcasted_iota(jnp.int32, (total, size), 1) + start
        first = start // units
        weight, sign = weights[first], signs[first]
        for later in range(first + 1, (start + size - 1) // units + 1):
            weight = jnp.where(column < later * units, weight, weights[later])
            sign = jnp.where(column < later * units, sign, signs[later])
        squash = jax.nn.sigmoid(pre_gate)
        act = pre_gate * squash
        hidden = act * pre_up
        sums = sums + jnp.sum(hidden * dhid * sign, axis=1, keepdims=True)
        dhid = dhid * weight
        dgate[:, span] = (dhid * pre_up * (squash + act * (1.0 - squash))).astype(BF16)
        dup[:, span] = (dhid * act).astype(BF16)
        hid[:, span] = (hidden * weight).astype(BF16)

    for at, d in ((at_0, d_0), (at_1, d_1)):
        there = pl.ds(at, half)
        mix = jnp.dot(hid[...], d[...], preferred_element_type=F32).astype(BF16)
        mix_own[:, there] = mix[:own]
        mix_a[:, there] = mix[own:own + sub]
        mix_b[:, there] = mix[own + sub:]

    high, low = split_low(sums)
    ends_ref[...] = jnp.where(lane == 0, high, jnp.where(lane == 1, low, 0.0)).astype(BF16)
    share = jnp.where(lane < count, extra + pltpu.roll(extra, EXT - count, 1), 0.0)
    dlogits = share * (1.0 - share) * pltpu.roll(extra, EXT - 2 * count, 1) * sums
    high, low = split_low(dlogits)
    sides = jnp.concatenate([high.T[:count], low.T[:count]], axis=0).astype(BF16)
    for at, r in ((at_0, r_0), (at_1, r_1)):
        routing = jnp.dot(sides, r[...], preferred_element_type=F32)
        routing_ref[:, pl.ds(at, half)] = routing[:count] + routing[count:]


def backward_kernel(
    tile,
    meta, dgate, dup, r_0, r_1, routing_ref, ends_ref, gate_0, gate_1, up_0, up_1,
    grad_own, grad_a, grad_b, params_ref,
    g_0, g_1, u_0, u_1, sems,
):
    half = gate_0.shape[1]
    own, sub = grad_own.shape[0], grad_a.shape[0]
    count = routing_ref.shape[0]
    width = 2 * half
    starts = (pl.multiple_of(meta[0] * half, half), pl.multiple_of((1 - meta[0]) * half, half))
    spots = ((0, gate_0, g_0, up_0, u_0, r_0), (1, gate_1, g_1, up_1, u_1, r_1))
    copies = []
    for which, gate, g, up, u, _ in spots:
        for number, (start, size) in enumerate(tiles_of(half, tile)):
            pair = []
            for kind, (source, target) in enumerate(((gate, g), (up, u))):
                copy = pltpu.make_async_copy(
                    source.at[:, pl.ds(start, size)], target.at[:, pl.ds(start, size)], sems.at[which, number, kind]
                )
                copy.start()
                pair.append(copy)
            copies.append(pair)
    ends = ends_ref[...]
    grad_own[:, width:] = ends[:own]
    grad_a[:, width:] = ends[own:own + sub]
    grad_b[:, width:] = ends[own + sub:]
    for which, _, g, _, u, r in spots:
        for start, size in tiles_of(half, tile):
            for copy in copies.pop(0):
                copy.wait()
            span = slice(start, start + size)
            grad = jnp.dot(dgate[...], g[:, span], preferred_element_type=F32) + jnp.dot(
                dup[...], u[:, span], preferred_element_type=F32
            )
            there = pl.ds(pl.multiple_of(starts[which] + start, EXT), size)
            low = grad.astype(BF16)
            grad_own[:, there] = low[:own]
            grad_a[:, there] = low[own:own + sub]
            grad_b[:, there] = low[own + sub:]
            moved = jnp.sum(grad * r[:, span].astype(F32), axis=0, keepdims=True)
            moved = jnp.broadcast_to(moved, (count, size))
            params_ref[:, there] = jnp.concatenate([routing_ref[:, there], moved], axis=0).astype(BF16)


def pack_kernel(
    mix_own, mix_a, mix_b, grad_own, grad_a, grad_b, sums_own, sums_core, sums_across, sums_diagonal, out_ref
):
    own, width = mix_own.shape
    sub = mix_a.shape[0]
    totals = (sums_own[...].astype(F32) + sums_core[...].astype(F32)) + (
        sums_across[...].astype(F32) + sums_diagonal[...].astype(F32)
    )
    lane = lanes(sub)
    upper, row = lanes(8) >= EXT // 2, lax.broadcasted_iota(jnp.int32, (8, EXT), 0)
    for begin, mix, grad in ((0, mix_a, grad_a), (sub, mix_b, grad_b)):
        span = slice(begin, begin + sub)
        out_ref[0, span, :width] = (mix_own[span, :].astype(F32) + mix[...].astype(F32)).astype(BF16)
        out_ref[1, span, :width] = (grad_own[span, :width].astype(F32) + grad[:, :width].astype(F32)).astype(BF16)
        both = grad_own[span, width:].astype(F32) + grad[:, width:].astype(F32)
        high, low = split_low(jnp.sum(both, axis=1, keepdims=True))
        gate_sums = jnp.where(lane == 0, high, jnp.where(lane == 1, low, 0.0))
        routing, ends = [], []
        for local in range(sub // 8):
            place = begin // 8 + local
            part = totals[:, place * EXT:(place + 1) * EXT]
            routing.append(part[:8])
            moved = jnp.where(row == 0, part[8:], jnp.where(row == 1, pltpu.roll(part[8:], EXT // 2, 1), 0.0))
            ends.append(jnp.where(upper, moved, gate_sums[8 * local:8 * local + 8]))
        out_ref[0, span, width:] = jnp.concatenate(routing, axis=0).astype(BF16)
        out_ref[1, span, width:] = jnp.concatenate(ends, axis=0).astype(BF16)


def finish_kernel(meta, parts_ref, x_ref, cot_ref, coef_ref, gain_ref, router_ref, out_ref):
    chunks = parts_ref.shape[0]
    width = x_ref.shape[2]
    total = parts_ref[0].astype(F32)
    for source in range(1, chunks):
        total = total + parts_ref[source].astype(F32)
    wide = x_ref[0].astype(F32)
    summed, extra = total[:, :width], total[:, width:]
    layer = wide + summed
    dlogits = coef_ref[0] * (extra[:, 0:1] + extra[:, 1:2])
    dnormed = summed
    for expert in range(router_ref.shape[0]):
        dnormed = dnormed + dlogits[:, expert:expert + 1] * router_ref[expert:expert + 1, :]
    scaling = inverse_rms(wide)
    unit = wide * scaling
    dunit = dnormed * gain_ref[...]
    dx = scaling * (dunit - unit * jnp.mean(dunit * unit, axis=-1, keepdims=True))
    grad = cot_ref[0].astype(F32) + dx
    out = jnp.where(meta[0] < chunks // 2, layer, grad).astype(BF16)
    ends = extra.astype(BF16)
    for place in range(chunks):
        out_ref[place, :, :width] = out
        out_ref[place, :, width:] = ends


def tail_kernel(all_ref, gain_ref, router_ref, layer_ref, grad_ref, grad_router_ref, grad_gain_ref):
    mid = all_ref.shape[0] // 2
    count, width = router_ref.shape
    layer_ref[...] = all_ref[:mid, :, :width]
    grad_ref[...] = all_ref[mid:, :, :width]
    upper = lanes(1) >= EXT // 2
    for place in range(mid):
        span = slice(place * EXT, (place + 1) * EXT)
        routing = all_ref[place, :, width:].astype(F32)
        ends = all_ref[mid + place, :, width:].astype(F32)
        moved = jnp.where(upper, ends[0:1], pltpu.roll(ends[1:2], EXT // 2, 1))
        grad_router_ref[:, span] = routing
        shares = jnp.sum(router_ref[:, span] * routing, axis=0, keepdims=True)
        grad_gain_ref[:, span] = (moved + shares) / gain_ref[:, span]


def whole(array):
    return pl.BlockSpec(array.shape, lambda *_: (0,) * len(array.shape))


def struct(*shape, dtype=BF16):
    return jax.ShapeDtypeStruct(shape, dtype)


def shards(n_dp, inputs, cotangent, w_gate, w_up, w_down, router, norm_gain, routes):
    micro, sub, width = inputs.shape
    own = micro * sub
    local, units, half = w_gate.shape
    count = router.shape[1]
    section, expert = lax.axis_index("section"), lax.axis_index("expert")
    place = lax.axis_index("dp")
    meta = jnp.stack([section, expert]).astype(jnp.int32)

    def around(shift):
        pairs = []
        for e in range(2):
            for d in range(n_dp):
                x = (d % 2 * 2 + e + shift) % 4
                pairs.append((e * n_dp + d, (x % 2) * n_dp + d - d % 2 + x // 2))
        return pairs

    def up_x(array):
        return lax.ppermute(array, ("expert", "dp"), around(1))

    def down_x(array):
        return lax.ppermute(array, ("expert", "dp"), around(3))

    def other_core(array):
        return lax.ppermute(array, "section", [(0, 1), (1, 0)])

    flat_x = inputs.reshape(own, width)
    flat_cot = cotangent.reshape(own, width)
    x_other, cot_other = up_x(flat_x), down_x(flat_cot)
    gate_0, up_0, down_0 = (w.reshape(local * units, half) for w in (w_gate, w_up, w_down))
    gate_1 = other_core(gate_0)
    up_1 = other_core(up_0)
    down_late, gate_1 = lax.optimization_barrier((down_0, gate_1))
    down_1 = other_core(down_late)
    maps = (gate_0, gate_1, up_0, up_1, down_0, down_1)
    gain_row = norm_gain.reshape(1, width)
    router_rows = router.T
    rows_own, extra_own, coef = pl.pallas_call(
        prologue_kernel,
        out_shape=(struct(own, width), struct(own, EXT), struct(own, EXT, dtype=F32)),
        compiler_params=params(WIDE_VMEM),
        cost_estimate=pl.CostEstimate(flops=20_000_000_000, bytes_accessed=2**25, transcendentals=0),
    )(flat_x, gain_row, router_rows, routes.reshape(own, 2))
    extra_other = up_x(extra_own)

    hidden_units = local * units
    near = pl.BlockSpec(memory_space=pltpu.VMEM)
    far = pl.BlockSpec(memory_space=pltpu.HBM)

    total = 2 * own
    scalar = pl.BlockSpec(memory_space=pltpu.SMEM)
    map_room = pltpu.VMEM((hidden_units, half), BF16)
    mix_own, mix_a, mix_b, dgate, dup, r_0, r_1, routing, ends = pl.pallas_call(
        functools.partial(forward_kernel, count, units, TILE),
        in_specs=[scalar] + [near] * 7 + [far] * 6,
        out_specs=(near,) * 9,
        out_shape=(
            struct(own, width), struct(sub, width), struct(sub, width),
            struct(total, hidden_units), struct(total, hidden_units), struct(total, half), struct(total, half),
            struct(count, width, dtype=F32), struct(total, EXT),
        ),
        scratch_shapes=[map_room] * 6
        + [pltpu.VMEM((total, half), BF16)] * 2
        + [pltpu.VMEM((total, hidden_units), BF16)]
        + [pltpu.SemaphoreType.DMA((len(tiles_of(hidden_units, TILE)), 6))],
        compiler_params=params(EXPERT_VMEM),
        cost_estimate=pl.CostEstimate(flops=2_000_000_000_000, bytes_accessed=1024, transcendentals=0),
    )(meta, rows_own, x_other, flat_cot, cot_other, extra_own, extra_other, gain_row, *maps)
    mix_a, mix_b = up_x(mix_a), down_x(mix_b)
    grad_own, grad_a, grad_b, sums = pl.pallas_call(
        functools.partial(backward_kernel, BACK_TILE),
        in_specs=[scalar] + [near] * 6 + [far] * 4,
        out_specs=(near,) * 4,
        out_shape=(
            struct(own, width + EXT), struct(sub, width + EXT), struct(sub, width + EXT), struct(2 * count, width),
        ),
        scratch_shapes=[map_room] * 4 + [pltpu.SemaphoreType.DMA((2, half // BACK_TILE, 2))],
        compiler_params=params(EXPERT_VMEM),
        cost_estimate=pl.CostEstimate(flops=1_000_000_000_000, bytes_accessed=1024, transcendentals=0),
    )(meta, dgate, dup, r_0, r_1, routing, ends, *maps[:4])
    mix_a, mix_b, grad_a, grad_b, sums = lax.optimization_barrier((mix_a, mix_b, grad_a, grad_b, sums))
    grad_a, grad_b = up_x(grad_a), down_x(grad_b)
    core = other_core(sums)
    across = lax.ppermute(sums, "expert", [(0, 1), (1, 0)])
    diagonal = lax.ppermute(sums, ("section", "expert"), [(0, 3), (1, 2), (2, 1), (3, 0)])
    packed = pl.pallas_call(
        pack_kernel, out_shape=struct(2, own, width + EXT), compiler_params=params()
    )(mix_own, mix_a, mix_b, grad_own, grad_a, grad_b, sums, core, across, diagonal)
    rows_each = 2 * own // n_dp
    chunks = lax.all_to_all(packed.reshape(n_dp, rows_each, width + EXT), "dp", 0, 0, tiled=True)

    blocks = own // rows_each
    spot = jnp.stack([place, place % blocks]).astype(jnp.int32)

    def at_spot(last):
        return pl.BlockSpec((1, rows_each, last), lambda i, m: (m[1], 0, 0))

    finished = pl.pallas_call(
        finish_kernel,
        grid_spec=pltpu.PrefetchScalarGridSpec(
            num_scalar_prefetch=1,
            grid=(1,),
            in_specs=[whole(chunks), at_spot(width), at_spot(width), at_spot(EXT), whole(gain_row), whole(router_rows)],
            out_specs=whole(chunks),
        ),
        out_shape=struct(*chunks.shape),
        compiler_params=params(),
    )(
        spot,
        chunks,
        inputs.reshape(blocks, rows_each, width),
        cotangent.reshape(blocks, rows_each, width),
        coef.reshape(blocks, rows_each, EXT),
        gain_row,
        router_rows,
    )
    gathered = lax.all_to_all(finished, "dp", 0, 0, tiled=True)

    layer, grad, grad_router, grad_gain = pl.pallas_call(
        tail_kernel,
        out_shape=(
            struct(blocks, rows_each, width), struct(blocks, rows_each, width),
            struct(count, width, dtype=F32), struct(1, width, dtype=F32),
        ),
        compiler_params=params(),
    )(gathered, gain_row, router_rows)
    return (
        layer.reshape(micro, sub, width), grad.reshape(micro, sub, width), grad_router.T, grad_gain.reshape(width)
    )


def solution(mesh):
    tokens = P(None, ("section", "expert"), None)
    maps = P("expert", "dp", "section")
    return jax.shard_map(
        functools.partial(shards, mesh.shape["dp"]),
        mesh=mesh,
        in_specs=(tokens, tokens, maps, maps, maps, P(), P(), tokens),
        out_specs=(tokens, tokens, P(), P()),
        check_vma=False,
    )
```

```python
import functools

import jax
import jax.numpy as jnp
from jax import lax
from jax.experimental import pallas as pl
from jax.experimental.pallas import tpu as pltpu
from jax.sharding import PartitionSpec as P

EPSILON = 1e-05
EXT = 128
F32 = jnp.float32
BF16 = jnp.bfloat16
HIGHEST = lax.Precision.HIGHEST
NT = (((1,), (1,)), ((), ()))
VMEM_BYTES = 16 * 1024 * 1024
EXPERT_VMEM = 41 * 1024 * 1024
BACK_VMEM = 16 * 1024 * 1024
WIDE_VMEM = 16 * 1024 * 1024
TILE = 256


def params(limit=VMEM_BYTES):
    return pltpu.CompilerParams(vmem_limit_bytes=limit)


def lanes(rows):
    return lax.broadcasted_iota(jnp.int32, (rows, EXT), 1)


def split_low(value):
    high = value.astype(BF16).astype(F32)
    return high, value - high


def inverse_rms(wide):
    return lax.rsqrt(jnp.mean(wide * wide, axis=-1, keepdims=True) + EPSILON)


def prologue_kernel(x_ref, gain_ref, router_ref, routes_ref, rows_ref, extra_ref, coef_ref):
    count = router_ref.shape[0]
    wide = x_ref[...].astype(F32)
    normed = wide * inverse_rms(wide) * gain_ref[...]
    rows_ref[...] = normed.astype(BF16)
    logits = lax.dot_general(normed, router_ref[...], NT, precision=HIGHEST, preferred_element_type=F32)
    first, second = routes_ref[:, 0:1], routes_ref[:, 1:2]
    column = lax.broadcasted_iota(jnp.int32, logits.shape, 1)
    signs = (column == first).astype(F32) - (column == second).astype(F32)
    leading = jax.nn.sigmoid(jnp.sum(signs * logits, axis=1, keepdims=True))
    trailing = 1.0 - leading
    lead_high, lead_low = split_low(leading)
    trail_high, trail_low = split_low(trailing)
    lane = lanes(x_ref.shape[0])

    def place(start, at_first, at_second):
        return jnp.where(lane == first + start, at_first, 0.0) + jnp.where(
            lane == second + start, at_second, 0.0
        )

    extra = (
        place(0, lead_high, trail_high)
        + place(count, lead_low, trail_low)
        + place(2 * count, 1.0, -1.0)
    )
    extra_ref[...] = extra.astype(BF16)
    slope = leading * trailing
    coef_ref[...] = place(0, slope, -slope)


def tiles_of(extent, size):
    starts = [0] + list(range(size // 2, extent, size))
    return [(start, min(end, extent) - start) for start, end in zip(starts, starts[1:] + [extent])]


def forward_kernel(
    count, units, tile,
    meta, rows_own, x_other, cot_own, cot_other, extra_own, extra_other, gain_ref,
    gate_0, gate_1, up_0, up_1, down_0, down_1,
    mix_own, mix_a, mix_b, dgate, dup, r_0, r_1, routing_ref, ends_ref, g_0, g_1, u_0, u_1,
    d_0, d_1, c_0, c_1, hid, sems,
):
    hidden_units, half = gate_0.shape
    own, sub = rows_own.shape[0], mix_a.shape[0]
    total = 2 * own
    local = hidden_units // units
    at_0 = pl.multiple_of(meta[0] * half, half)
    at_1 = pl.multiple_of((1 - meta[0]) * half, half)
    tiles = tiles_of(hidden_units, tile)

    def fetch(number):
        start, size = tiles[number]
        group = []
        for which, (source, target) in enumerate(
            ((gate_0, g_0), (gate_1, g_1), (up_0, u_0), (up_1, u_1), (down_0, d_0), (down_1, d_1))
        ):
            copy = pltpu.make_async_copy(
                source.at[pl.ds(start, size), :], target.at[pl.ds(start, size), :], sems.at[number, which]
            )
            copy.start()
            group.append(copy)
        return group

    copies = [fetch(0), fetch(1)]
    scaling = inverse_rms(x_other[...].astype(F32))
    for at, r, c in ((at_0, r_0, c_0), (at_1, r_1, c_1)):
        there = pl.ds(at, half)
        r[:own, :] = rows_own[:, there]
        r[own:, :] = (x_other[:, there].astype(F32) * scaling * gain_ref[:, there]).astype(BF16)
        c[:own, :] = cot_own[:, there]
        c[own:, :] = cot_other[:, there]

    lane = lanes(total)
    extra = jnp.concatenate([extra_own[...], extra_other[...]], axis=0).astype(F32)
    weights, signs = [], []
    for which in range(local):
        expert = meta[1] * local + which
        weights.append(
            jnp.sum(jnp.where((lane == expert) | (lane == expert + count), extra, 0.0), axis=1, keepdims=True)
        )
        signs.append(jnp.sum(jnp.where(lane == expert + 2 * count, extra, 0.0), axis=1, keepdims=True))

    def products(number):
        if number + 2 < len(tiles):
            copies.append(fetch(number + 2))
        for copy in copies[number]:
            copy.wait()
        start, size = tiles[number]
        span = slice(start, start + size)

        def both(left_0, left_1, map_0, map_1):
            return lax.dot_general(left_0[...], map_0[span, :], NT, preferred_element_type=F32) + lax.dot_general(
                left_1[...], map_1[span, :], NT, preferred_element_type=F32
            )

        return both(r_0, r_1, g_0, g_1), both(r_0, r_1, u_0, u_1), both(c_0, c_1, d_0, d_1)

    sums = jnp.zeros((total, 1), F32)
    ahead = products(0)
    for number, (start, size) in enumerate(tiles):
        pre_gate, pre_up, dhid = ahead
        if number + 1 < len(tiles):
            ahead = products(number + 1)
        span = slice(start, start + size)
        column = lax.broadcasted_iota(jnp.int32, (total, size), 1) + start
        first = start // units
        weight, sign = weights[first], signs[first]
        for later in range(first + 1, (start + size - 1) // units + 1):
            weight = jnp.where(column < later * units, weight, weights[later])
            sign = jnp.where(column < later * units, sign, signs[later])
        squash = jax.nn.sigmoid(pre_gate)
        act = pre_gate * squash
        hidden = act * pre_up
        sums = sums + jnp.sum(hidden * dhid * sign, axis=1, keepdims=True)
        dhid = dhid * weight
        dgate[:, span] = (dhid * pre_up * (squash + act * (1.0 - squash))).astype(BF16)
        dup[:, span] = (dhid * act).astype(BF16)
        hid[:, span] = (hidden * weight).astype(BF16)

    for at, d in ((at_0, d_0), (at_1, d_1)):
        there = pl.ds(at, half)
        mix = jnp.dot(hid[...], d[...], preferred_element_type=F32).astype(BF16)
        mix_own[:, there] = mix[:own]
        mix_a[:, there] = mix[own:own + sub]
        mix_b[:, there] = mix[own + sub:]

    high, low = split_low(sums)
    ends_ref[...] = jnp.where(lane == 0, high, jnp.where(lane == 1, low, 0.0)).astype(BF16)
    share = jnp.where(lane < count, extra + pltpu.roll(extra, EXT - count, 1), 0.0)
    dlogits = share * (1.0 - share) * pltpu.roll(extra, EXT - 2 * count, 1) * sums
    high, low = split_low(dlogits)
    sides = jnp.concatenate([high.T[:count], low.T[:count]], axis=0).astype(BF16)
    for at, r in ((at_0, r_0), (at_1, r_1)):
        routing = jnp.dot(sides, r[...], preferred_element_type=F32)
        routing_ref[:, pl.ds(at, half)] = routing[:count] + routing[count:]


def backward_kernel(
    meta, dgate, dup, r_0, r_1, routing_ref, ends_ref, g_0, g_1, u_0, u_1, grad_own, grad_a, grad_b, params_ref
):
    half = g_0.shape[1]
    own, sub = grad_own.shape[0], grad_a.shape[0]
    count = routing_ref.shape[0]
    ends = ends_ref[...]
    grad_own[:, 2 * half:] = ends[:own]
    grad_a[:, 2 * half:] = ends[own:own + sub]
    grad_b[:, 2 * half:] = ends[own + sub:]
    for at, g, u, r in ((meta[0], g_0, u_0, r_0), (1 - meta[0], g_1, u_1, r_1)):
        there = pl.ds(pl.multiple_of(at * half, half), half)
        grad = jnp.dot(dgate[...], g[...], preferred_element_type=F32) + jnp.dot(
            dup[...], u[...], preferred_element_type=F32
        )
        low = grad.astype(BF16)
        grad_own[:, there] = low[:own]
        grad_a[:, there] = low[own:own + sub]
        grad_b[:, there] = low[own + sub:]
        moved = jnp.sum(grad * r[...].astype(F32), axis=0, keepdims=True)
        moved = jnp.broadcast_to(moved, (count, half))
        params_ref[:, there] = jnp.concatenate([routing_ref[:, there], moved], axis=0)


def pack_kernel(
    mix_own, mix_a, mix_b, grad_own, grad_a, grad_b, sums_own, sums_across, out_ref
):
    own, width = mix_own.shape
    sub = mix_a.shape[0]
    totals = sums_own[...].astype(F32) + sums_across[...].astype(F32)
    lane = lanes(sub)
    upper, row = lanes(8) >= EXT // 2, lax.broadcasted_iota(jnp.int32, (8, EXT), 0)
    for begin, mix, grad in ((0, mix_a, grad_a), (sub, mix_b, grad_b)):
        span = slice(begin, begin + sub)
        out_ref[0, span, :width] = (mix_own[span, :].astype(F32) + mix[...].astype(F32)).astype(BF16)
        out_ref[1, span, :width] = (grad_own[span, :width].astype(F32) + grad[:, :width].astype(F32)).astype(BF16)
        both = grad_own[span, width:].astype(F32) + grad[:, width:].astype(F32)
        high, low = split_low(jnp.sum(both, axis=1, keepdims=True))
        gate_sums = jnp.where(lane == 0, high, jnp.where(lane == 1, low, 0.0))
        routing, ends = [], []
        for local in range(sub // 8):
            place = begin // 8 + local
            part = totals[:, place * EXT:(place + 1) * EXT]
            routing.append(part[:8])
            moved = jnp.where(row == 0, part[8:], jnp.where(row == 1, pltpu.roll(part[8:], EXT // 2, 1), 0.0))
            ends.append(jnp.where(upper, moved, gate_sums[8 * local:8 * local + 8]))
        out_ref[0, span, width:] = jnp.concatenate(routing, axis=0).astype(BF16)
        out_ref[1, span, width:] = jnp.concatenate(ends, axis=0).astype(BF16)


def finish_kernel(meta, parts_ref, x_ref, cot_ref, coef_ref, gain_ref, router_ref, out_ref):
    chunks = parts_ref.shape[0]
    width = x_ref.shape[2]
    total = parts_ref[0].astype(F32)
    for source in range(1, chunks):
        total = total + parts_ref[source].astype(F32)
    wide = x_ref[0].astype(F32)
    summed, extra = total[:, :width], total[:, width:]
    layer = wide + summed
    dlogits = coef_ref[0] * (extra[:, 0:1] + extra[:, 1:2])
    dnormed = summed
    for expert in range(router_ref.shape[0]):
        dnormed = dnormed + dlogits[:, expert:expert + 1] * router_ref[expert:expert + 1, :]
    scaling = inverse_rms(wide)
    unit = wide * scaling
    dunit = dnormed * gain_ref[...]
    dx = scaling * (dunit - unit * jnp.mean(dunit * unit, axis=-1, keepdims=True))
    grad = cot_ref[0].astype(F32) + dx
    out = jnp.where(meta[0] < chunks // 2, layer, grad).astype(BF16)
    ends = extra.astype(BF16)
    for place in range(chunks):
        out_ref[place, :, :width] = out
        out_ref[place, :, width:] = ends


def tail_kernel(all_ref, gain_ref, router_ref, layer_ref, grad_ref, grad_router_ref, grad_gain_ref):
    mid = all_ref.shape[0] // 2
    count, width = router_ref.shape
    layer_ref[...] = all_ref[:mid, :, :width]
    grad_ref[...] = all_ref[mid:, :, :width]
    upper = lanes(1) >= EXT // 2
    for place in range(mid):
        span = slice(place * EXT, (place + 1) * EXT)
        routing = all_ref[place, :, width:].astype(F32)
        ends = all_ref[mid + place, :, width:].astype(F32)
        moved = jnp.where(upper, ends[0:1], pltpu.roll(ends[1:2], EXT // 2, 1))
        grad_router_ref[:, span] = routing
        shares = jnp.sum(router_ref[:, span] * routing, axis=0, keepdims=True)
        grad_gain_ref[:, span] = (moved + shares) / gain_ref[:, span]


def whole(array):
    return pl.BlockSpec(array.shape, lambda *_: (0,) * len(array.shape))


def struct(*shape, dtype=BF16):
    return jax.ShapeDtypeStruct(shape, dtype)


def shards(n_dp, inputs, cotangent, w_gate, w_up, w_down, router, norm_gain, routes):
    micro, sub, width = inputs.shape
    own = micro * sub
    local, units, half = w_gate.shape
    count = router.shape[1]
    section, expert = lax.axis_index("section"), lax.axis_index("expert")
    place = lax.axis_index("dp")
    meta = jnp.stack([section, expert]).astype(jnp.int32)

    def around(shift):
        pairs = []
        for e in range(2):
            for d in range(n_dp):
                x = (d % 2 * 2 + e + shift) % 4
                pairs.append((e * n_dp + d, (x % 2) * n_dp + d - d % 2 + x // 2))
        return pairs

    def up_x(array):
        return lax.ppermute(array, ("expert", "dp"), around(1))

    def down_x(array):
        return lax.ppermute(array, ("expert", "dp"), around(3))

    def other_core(array):
        return lax.ppermute(array, "section", [(0, 1), (1, 0)])

    flat_x = inputs.reshape(own, width)
    flat_cot = cotangent.reshape(own, width)
    x_other, cot_other = up_x(flat_x), down_x(flat_cot)
    gate_0, up_0, down_0 = (w.reshape(local * units, half) for w in (w_gate, w_up, w_down))
    gate_1 = other_core(gate_0)
    up_1 = other_core(up_0)
    down_late, gate_1 = lax.optimization_barrier((down_0, gate_1))
    down_1 = other_core(down_late)
    maps = (gate_0, gate_1, up_0, up_1, down_0, down_1)
    gain_row = norm_gain.reshape(1, width)
    router_rows = router.T
    rows_own, extra_own, coef = pl.pallas_call(
        prologue_kernel,
        out_shape=(struct(own, width), struct(own, EXT), struct(own, EXT, dtype=F32)),
        compiler_params=params(WIDE_VMEM),
        cost_estimate=pl.CostEstimate(flops=20_000_000_000, bytes_accessed=2**25, transcendentals=0),
    )(flat_x, gain_row, router_rows, routes.reshape(own, 2))
    extra_other = up_x(extra_own)

    hidden_units = local * units
    near = pl.BlockSpec(memory_space=pltpu.VMEM)
    far = pl.BlockSpec(memory_space=pltpu.HBM)

    total = 2 * own
    scalar = pl.BlockSpec(memory_space=pltpu.SMEM)
    map_room = pltpu.VMEM((hidden_units, half), BF16)
    mix_own, mix_a, mix_b, dgate, dup, r_0, r_1, routing, ends, *held = pl.pallas_call(
        functools.partial(forward_kernel, count, units, TILE),
        in_specs=[scalar] + [near] * 7 + [far] * 6,
        out_specs=(near,) * 13,
        out_shape=(
            struct(own, width), struct(sub, width), struct(sub, width),
            struct(total, hidden_units), struct(total, hidden_units), struct(total, half), struct(total, half),
            struct(count, width, dtype=F32), struct(total, EXT),
        )
        + (struct(hidden_units, half),) * 4,
        scratch_shapes=[map_room] * 2
        + [pltpu.VMEM((total, half), BF16)] * 2
        + [pltpu.VMEM((total, hidden_units), BF16)]
        + [pltpu.SemaphoreType.DMA((len(tiles_of(hidden_units, TILE)), 6))],
        compiler_params=params(EXPERT_VMEM),
        cost_estimate=pl.CostEstimate(flops=2_000_000_000_000, bytes_accessed=1024, transcendentals=0),
    )(meta, rows_own, x_other, flat_cot, cot_other, extra_own, extra_other, gain_row, *maps)
    mix_a, mix_b = up_x(mix_a), down_x(mix_b)
    grad_own, grad_a, grad_b, sums = pl.pallas_call(
        backward_kernel,
        in_specs=[scalar] + [near] * 10,
        out_specs=(near,) * 4,
        out_shape=(
            struct(own, width + EXT), struct(sub, width + EXT), struct(sub, width + EXT),
            struct(2 * count, width, dtype=F32),
        ),
        compiler_params=params(BACK_VMEM),
        cost_estimate=pl.CostEstimate(flops=1_000_000_000_000, bytes_accessed=1024, transcendentals=0),
    )(meta, dgate, dup, r_0, r_1, routing, ends, *held)
    mix_a, mix_b, grad_a, grad_b = lax.optimization_barrier((mix_a, mix_b, grad_a, grad_b))
    grad_a, grad_b = up_x(grad_a), down_x(grad_b)
    sums = (sums + other_core(sums)).astype(BF16)
    across = lax.ppermute(sums, "expert", [(0, 1), (1, 0)])
    packed = pl.pallas_call(
        pack_kernel, out_shape=struct(2, own, width + EXT), compiler_params=params()
    )(mix_own, mix_a, mix_b, grad_own, grad_a, grad_b, sums, across)
    rows_each = 2 * own // n_dp
    chunks = lax.all_to_all(packed.reshape(n_dp, rows_each, width + EXT), "dp", 0, 0, tiled=True)

    blocks = own // rows_each
    spot = jnp.stack([place, place % blocks]).astype(jnp.int32)

    def at_spot(last):
        return pl.BlockSpec((1, rows_each, last), lambda i, m: (m[1], 0, 0))

    finished = pl.pallas_call(
        finish_kernel,
        grid_spec=pltpu.PrefetchScalarGridSpec(
            num_scalar_prefetch=1,
            grid=(1,),
            in_specs=[whole(chunks), at_spot(width), at_spot(width), at_spot(EXT), whole(gain_row), whole(router_rows)],
            out_specs=whole(chunks),
        ),
        out_shape=struct(*chunks.shape),
        compiler_params=params(),
    )(
        spot,
        chunks,
        inputs.reshape(blocks, rows_each, width),
        cotangent.reshape(blocks, rows_each, width),
        coef.reshape(blocks, rows_each, EXT),
        gain_row,
        router_rows,
    )
    gathered = lax.all_to_all(finished, "dp", 0, 0, tiled=True)

    layer, grad, grad_router, grad_gain = pl.pallas_call(
        tail_kernel,
        out_shape=(
            struct(blocks, rows_each, width), struct(blocks, rows_each, width),
            struct(count, width, dtype=F32), struct(1, width, dtype=F32),
        ),
        compiler_params=params(),
    )(gathered, gain_row, router_rows)
    return (
        layer.reshape(micro, sub, width), grad.reshape(micro, sub, width), grad_router.T, grad_gain.reshape(width)
    )


def solution(mesh):
    tokens = P(None, ("section", "expert"), None)
    maps = P("expert", "dp", "section")
    return jax.shard_map(
        functools.partial(shards, mesh.shape["dp"]),
        mesh=mesh,
        in_specs=(tokens, tokens, maps, maps, maps, P(), P(), tokens),
        out_specs=(tokens, tokens, P(), P()),
        check_vma=False,
    )
```

```python
import functools

import jax
import jax.numpy as jnp
from jax import lax
from jax.experimental import pallas as pl
from jax.experimental.pallas import tpu as pltpu
from jax.sharding import PartitionSpec as P

EPSILON = 1e-05
EXT = 128
F32 = jnp.float32
BF16 = jnp.bfloat16
HIGHEST = lax.Precision.HIGHEST
NT = (((1,), (1,)), ((), ()))
VMEM_BYTES = 16 * 1024 * 1024
EXPERT_VMEM = 41 * 1024 * 1024
BACK_VMEM = 16 * 1024 * 1024
WIDE_VMEM = 16 * 1024 * 1024
TILE = 256


def params(limit=VMEM_BYTES):
    return pltpu.CompilerParams(vmem_limit_bytes=limit)


def lanes(rows):
    return lax.broadcasted_iota(jnp.int32, (rows, EXT), 1)


def split_low(value):
    high = value.astype(BF16).astype(F32)
    return high, value - high


def inverse_rms(wide):
    return lax.rsqrt(jnp.mean(wide * wide, axis=-1, keepdims=True) + EPSILON)


def prologue_kernel(x_ref, gain_ref, router_ref, routes_ref, rows_ref, extra_ref, coef_ref):
    count = router_ref.shape[0]
    wide = x_ref[...].astype(F32)
    normed = wide * inverse_rms(wide) * gain_ref[...]
    rows_ref[...] = normed.astype(BF16)
    logits = lax.dot_general(normed, router_ref[...], NT, precision=HIGHEST, preferred_element_type=F32)
    first, second = routes_ref[:, 0:1], routes_ref[:, 1:2]
    column = lax.broadcasted_iota(jnp.int32, logits.shape, 1)
    signs = (column == first).astype(F32) - (column == second).astype(F32)
    leading = jax.nn.sigmoid(jnp.sum(signs * logits, axis=1, keepdims=True))
    trailing = 1.0 - leading
    lead_high, lead_low = split_low(leading)
    trail_high, trail_low = split_low(trailing)
    lane = lanes(x_ref.shape[0])

    def place(start, at_first, at_second):
        return jnp.where(lane == first + start, at_first, 0.0) + jnp.where(
            lane == second + start, at_second, 0.0
        )

    extra = (
        place(0, lead_high, trail_high)
        + place(count, lead_low, trail_low)
        + place(2 * count, 1.0, -1.0)
    )
    extra_ref[...] = extra.astype(BF16)
    slope = leading * trailing
    coef_ref[...] = place(0, slope, -slope)


def tiles_of(extent, size):
    starts = [0] + list(range(size // 2, extent, size))
    return [(start, min(end, extent) - start) for start, end in zip(starts, starts[1:] + [extent])]


def forward_kernel(
    count, units, tile,
    meta, rows_own, x_other, cot_own, cot_other, extra_own, extra_other, gain_ref,
    gate_0, gate_1, up_0, up_1, down_0, down_1,
    mix_own, mix_a, mix_b, dgate, dup, r_0, r_1, routing_ref, ends_ref, g_0, g_1, u_0, u_1,
    d_0, d_1, c_0, c_1, hid, sems,
):
    hidden_units, half = gate_0.shape
    own, sub = rows_own.shape[0], mix_a.shape[0]
    total = 2 * own
    local = hidden_units // units
    at_0 = pl.multiple_of(meta[0] * half, half)
    at_1 = pl.multiple_of((1 - meta[0]) * half, half)
    tiles = tiles_of(hidden_units, tile)

    def fetch(number):
        start, size = tiles[number]
        group = []
        for which, (source, target) in enumerate(
            ((gate_0, g_0), (gate_1, g_1), (up_0, u_0), (up_1, u_1), (down_0, d_0), (down_1, d_1))
        ):
            copy = pltpu.make_async_copy(
                source.at[pl.ds(start, size), :], target.at[pl.ds(start, size), :], sems.at[number, which]
            )
            copy.start()
            group.append(copy)
        return group

    copies = [fetch(number) for number in range(len(tiles))]
    scaling = inverse_rms(x_other[...].astype(F32))
    for at, r, c in ((at_0, r_0, c_0), (at_1, r_1, c_1)):
        there = pl.ds(at, half)
        r[:own, :] = rows_own[:, there]
        r[own:, :] = (x_other[:, there].astype(F32) * scaling * gain_ref[:, there]).astype(BF16)
        c[:own, :] = cot_own[:, there]
        c[own:, :] = cot_other[:, there]

    lane = lanes(total)
    extra = jnp.concatenate([extra_own[...], extra_other[...]], axis=0).astype(F32)
    weights, signs = [], []
    for which in range(local):
        expert = meta[1] * local + which
        weights.append(
            jnp.sum(jnp.where((lane == expert) | (lane == expert + count), extra, 0.0), axis=1, keepdims=True)
        )
        signs.append(jnp.sum(jnp.where(lane == expert + 2 * count, extra, 0.0), axis=1, keepdims=True))

    def products(number):
        for copy in copies[number]:
            copy.wait()
        start, size = tiles[number]
        span = slice(start, start + size)

        def both(left_0, left_1, map_0, map_1):
            return lax.dot_general(left_0[...], map_0[span, :], NT, preferred_element_type=F32) + lax.dot_general(
                left_1[...], map_1[span, :], NT, preferred_element_type=F32
            )

        return both(r_0, r_1, g_0, g_1), both(r_0, r_1, u_0, u_1), both(c_0, c_1, d_0, d_1)

    sums = jnp.zeros((total, 1), F32)
    ahead = products(0)
    for number, (start, size) in enumerate(tiles):
        pre_gate, pre_up, dhid = ahead
        if number + 1 < len(tiles):
            ahead = products(number + 1)
        span = slice(start, start + size)
        column = lax.broadcasted_iota(jnp.int32, (total, size), 1) + start
        first = start // units
        weight, sign = weights[first], signs[first]
        for later in range(first + 1, (start + size - 1) // units + 1):
            weight = jnp.where(column < later * units, weight, weights[later])
            sign = jnp.where(column < later * units, sign, signs[later])
        squash = jax.nn.sigmoid(pre_gate)
        act = pre_gate * squash
        hidden = act * pre_up
        sums = sums + jnp.sum(hidden * dhid * sign, axis=1, keepdims=True)
        dhid = dhid * weight
        dgate[:, span] = (dhid * pre_up * (squash + act * (1.0 - squash))).astype(BF16)
        dup[:, span] = (dhid * act).astype(BF16)
        hid[:, span] = (hidden * weight).astype(BF16)

    for at, d in ((at_0, d_0), (at_1, d_1)):
        there = pl.ds(at, half)
        mix = jnp.dot(hid[...], d[...], preferred_element_type=F32).astype(BF16)
        mix_own[:, there] = mix[:own]
        mix_a[:, there] = mix[own:own + sub]
        mix_b[:, there] = mix[own + sub:]

    high, low = split_low(sums)
    ends_ref[...] = jnp.where(lane == 0, high, jnp.where(lane == 1, low, 0.0)).astype(BF16)
    share = jnp.where(lane < count, extra + pltpu.roll(extra, EXT - count, 1), 0.0)
    dlogits = share * (1.0 - share) * pltpu.roll(extra, EXT - 2 * count, 1) * sums
    high, low = split_low(dlogits)
    sides = jnp.concatenate([high.T[:count], low.T[:count]], axis=0).astype(BF16)
    for at, r in ((at_0, r_0), (at_1, r_1)):
        routing = jnp.dot(sides, r[...], preferred_element_type=F32)
        routing_ref[:, pl.ds(at, half)] = routing[:count] + routing[count:]


def backward_kernel(
    meta, dgate, dup, r_0, r_1, routing_ref, ends_ref, g_0, g_1, u_0, u_1, grad_own, grad_a, grad_b, params_ref
):
    half = g_0.shape[1]
    own, sub = grad_own.shape[0], grad_a.shape[0]
    count = routing_ref.shape[0]
    ends = ends_ref[...]
    grad_own[:, 2 * half:] = ends[:own]
    grad_a[:, 2 * half:] = ends[own:own + sub]
    grad_b[:, 2 * half:] = ends[own + sub:]
    for at, g, u, r in ((meta[0], g_0, u_0, r_0), (1 - meta[0], g_1, u_1, r_1)):
        there = pl.ds(pl.multiple_of(at * half, half), half)
        grad = jnp.dot(dgate[...], g[...], preferred_element_type=F32) + jnp.dot(
            dup[...], u[...], preferred_element_type=F32
        )
        low = grad.astype(BF16)
        grad_own[:, there] = low[:own]
        grad_a[:, there] = low[own:own + sub]
        grad_b[:, there] = low[own + sub:]
        moved = jnp.sum(grad * r[...].astype(F32), axis=0, keepdims=True)
        moved = jnp.broadcast_to(moved, (count, half))
        params_ref[:, there] = jnp.concatenate([routing_ref[:, there], moved], axis=0)


def pack_kernel(
    mix_own, mix_a, mix_b, grad_own, grad_a, grad_b, sums_own, sums_across, out_ref
):
    own, width = mix_own.shape
    sub = mix_a.shape[0]
    totals = sums_own[...].astype(F32) + sums_across[...].astype(F32)
    lane = lanes(sub)
    upper, row = lanes(8) >= EXT // 2, lax.broadcasted_iota(jnp.int32, (8, EXT), 0)
    for begin, mix, grad in ((0, mix_a, grad_a), (sub, mix_b, grad_b)):
        span = slice(begin, begin + sub)
        out_ref[0, span, :width] = (mix_own[span, :].astype(F32) + mix[...].astype(F32)).astype(BF16)
        out_ref[1, span, :width] = (grad_own[span, :width].astype(F32) + grad[:, :width].astype(F32)).astype(BF16)
        both = grad_own[span, width:].astype(F32) + grad[:, width:].astype(F32)
        high, low = split_low(jnp.sum(both, axis=1, keepdims=True))
        gate_sums = jnp.where(lane == 0, high, jnp.where(lane == 1, low, 0.0))
        routing, ends = [], []
        for local in range(sub // 8):
            place = begin // 8 + local
            part = totals[:, place * EXT:(place + 1) * EXT]
            routing.append(part[:8])
            moved = jnp.where(row == 0, part[8:], jnp.where(row == 1, pltpu.roll(part[8:], EXT // 2, 1), 0.0))
            ends.append(jnp.where(upper, moved, gate_sums[8 * local:8 * local + 8]))
        out_ref[0, span, width:] = jnp.concatenate(routing, axis=0).astype(BF16)
        out_ref[1, span, width:] = jnp.concatenate(ends, axis=0).astype(BF16)


def finish_kernel(meta, parts_ref, x_ref, cot_ref, coef_ref, gain_ref, router_ref, out_ref):
    chunks = parts_ref.shape[0]
    width = x_ref.shape[2]
    total = parts_ref[0].astype(F32)
    for source in range(1, chunks):
        total = total + parts_ref[source].astype(F32)
    wide = x_ref[0].astype(F32)
    summed, extra = total[:, :width], total[:, width:]
    layer = wide + summed
    dlogits = coef_ref[0] * (extra[:, 0:1] + extra[:, 1:2])
    dnormed = summed
    for expert in range(router_ref.shape[0]):
        dnormed = dnormed + dlogits[:, expert:expert + 1] * router_ref[expert:expert + 1, :]
    scaling = inverse_rms(wide)
    unit = wide * scaling
    dunit = dnormed * gain_ref[...]
    dx = scaling * (dunit - unit * jnp.mean(dunit * unit, axis=-1, keepdims=True))
    grad = cot_ref[0].astype(F32) + dx
    out = jnp.where(meta[0] < chunks // 2, layer, grad).astype(BF16)
    ends = extra.astype(BF16)
    for place in range(chunks):
        out_ref[place, :, :width] = out
        out_ref[place, :, width:] = ends


def tail_kernel(all_ref, gain_ref, router_ref, layer_ref, grad_ref, grad_router_ref, grad_gain_ref):
    mid = all_ref.shape[0] // 2
    count, width = router_ref.shape
    layer_ref[...] = all_ref[:mid, :, :width]
    grad_ref[...] = all_ref[mid:, :, :width]
    upper = lanes(1) >= EXT // 2
    for place in range(mid):
        span = slice(place * EXT, (place + 1) * EXT)
        routing = all_ref[place, :, width:].astype(F32)
        ends = all_ref[mid + place, :, width:].astype(F32)
        moved = jnp.where(upper, ends[0:1], pltpu.roll(ends[1:2], EXT // 2, 1))
        grad_router_ref[:, span] = routing
        shares = jnp.sum(router_ref[:, span] * routing, axis=0, keepdims=True)
        grad_gain_ref[:, span] = (moved + shares) / gain_ref[:, span]


def whole(array):
    return pl.BlockSpec(array.shape, lambda *_: (0,) * len(array.shape))


def struct(*shape, dtype=BF16):
    return jax.ShapeDtypeStruct(shape, dtype)


def shards(n_dp, inputs, cotangent, w_gate, w_up, w_down, router, norm_gain, routes):
    micro, sub, width = inputs.shape
    own = micro * sub
    local, units, half = w_gate.shape
    count = router.shape[1]
    section, expert = lax.axis_index("section"), lax.axis_index("expert")
    place = lax.axis_index("dp")
    meta = jnp.stack([section, expert]).astype(jnp.int32)

    def around(shift):
        pairs = []
        for e in range(2):
            for d in range(n_dp):
                x = (d % 2 * 2 + e + shift) % 4
                pairs.append((e * n_dp + d, (x % 2) * n_dp + d - d % 2 + x // 2))
        return pairs

    def up_x(array):
        return lax.ppermute(array, ("expert", "dp"), around(1))

    def down_x(array):
        return lax.ppermute(array, ("expert", "dp"), around(3))

    def other_core(array):
        return lax.ppermute(array, "section", [(0, 1), (1, 0)])

    flat_x = inputs.reshape(own, width)
    flat_cot = cotangent.reshape(own, width)
    x_other, cot_other = up_x(flat_x), down_x(flat_cot)
    gate_0, up_0, down_0 = (w.reshape(local * units, half) for w in (w_gate, w_up, w_down))
    gate_1 = other_core(gate_0)
    up_1 = other_core(up_0)
    down_late, gate_1 = lax.optimization_barrier((down_0, gate_1))
    down_1 = other_core(down_late)
    maps = (gate_0, gate_1, up_0, up_1, down_0, down_1)
    gain_row = norm_gain.reshape(1, width)
    router_rows = router.T
    rows_own, extra_own, coef = pl.pallas_call(
        prologue_kernel,
        out_shape=(struct(own, width), struct(own, EXT), struct(own, EXT, dtype=F32)),
        compiler_params=params(WIDE_VMEM),
        cost_estimate=pl.CostEstimate(flops=20_000_000_000, bytes_accessed=2**25, transcendentals=0),
    )(flat_x, gain_row, router_rows, routes.reshape(own, 2))
    extra_other = up_x(extra_own)

    hidden_units = local * units
    near = pl.BlockSpec(memory_space=pltpu.VMEM)
    far = pl.BlockSpec(memory_space=pltpu.HBM)

    total = 2 * own
    scalar = pl.BlockSpec(memory_space=pltpu.SMEM)
    map_room = pltpu.VMEM((hidden_units, half), BF16)
    mix_own, mix_a, mix_b, dgate, dup, r_0, r_1, routing, ends, *held = pl.pallas_call(
        functools.partial(forward_kernel, count, units, TILE),
        in_specs=[scalar] + [near] * 7 + [far] * 6,
        out_specs=(near,) * 13,
        out_shape=(
            struct(own, width), struct(sub, width), struct(sub, width),
            struct(total, hidden_units), struct(total, hidden_units), struct(total, half), struct(total, half),
            struct(count, width, dtype=F32), struct(total, EXT),
        )
        + (struct(hidden_units, half),) * 4,
        scratch_shapes=[map_room] * 2
        + [pltpu.VMEM((total, half), BF16)] * 2
        + [pltpu.VMEM((total, hidden_units), BF16)]
        + [pltpu.SemaphoreType.DMA((len(tiles_of(hidden_units, TILE)), 6))],
        compiler_params=params(EXPERT_VMEM),
        cost_estimate=pl.CostEstimate(flops=2_000_000_000_000, bytes_accessed=1024, transcendentals=0),
    )(meta, rows_own, x_other, flat_cot, cot_other, extra_own, extra_other, gain_row, *maps)
    mix_a, mix_b = up_x(mix_a), down_x(mix_b)
    grad_own, grad_a, grad_b, sums = pl.pallas_call(
        backward_kernel,
        in_specs=[scalar] + [near] * 10,
        out_specs=(near,) * 4,
        out_shape=(
            struct(own, width + EXT), struct(sub, width + EXT), struct(sub, width + EXT),
            struct(2 * count, width, dtype=F32),
        ),
        compiler_params=params(BACK_VMEM),
        cost_estimate=pl.CostEstimate(flops=20_000_000_000, bytes_accessed=1024, transcendentals=0),
    )(meta, dgate, dup, r_0, r_1, routing, ends, *held)
    mix_a, mix_b, grad_a, grad_b = lax.optimization_barrier((mix_a, mix_b, grad_a, grad_b))
    grad_a, grad_b = up_x(grad_a), down_x(grad_b)
    sums = (sums + other_core(sums)).astype(BF16)
    across = lax.ppermute(sums, "expert", [(0, 1), (1, 0)])
    packed = pl.pallas_call(
        pack_kernel, out_shape=struct(2, own, width + EXT), compiler_params=params()
    )(mix_own, mix_a, mix_b, grad_own, grad_a, grad_b, sums, across)
    rows_each = 2 * own // n_dp
    chunks = lax.all_to_all(packed.reshape(n_dp, rows_each, width + EXT), "dp", 0, 0, tiled=True)

    blocks = own // rows_each
    spot = jnp.stack([place, place % blocks]).astype(jnp.int32)

    def at_spot(last):
        return pl.BlockSpec((1, rows_each, last), lambda i, m: (m[1], 0, 0))

    finished = pl.pallas_call(
        finish_kernel,
        grid_spec=pltpu.PrefetchScalarGridSpec(
            num_scalar_prefetch=1,
            grid=(1,),
            in_specs=[whole(chunks), at_spot(width), at_spot(width), at_spot(EXT), whole(gain_row), whole(router_rows)],
            out_specs=whole(chunks),
        ),
        out_shape=struct(*chunks.shape),
        compiler_params=params(),
    )(
        spot,
        chunks,
        inputs.reshape(blocks, rows_each, width),
        cotangent.reshape(blocks, rows_each, width),
        coef.reshape(blocks, rows_each, EXT),
        gain_row,
        router_rows,
    )
    gathered = lax.all_to_all(finished, "dp", 0, 0, tiled=True)

    layer, grad, grad_router, grad_gain = pl.pallas_call(
        tail_kernel,
        out_shape=(
            struct(blocks, rows_each, width), struct(blocks, rows_each, width),
            struct(count, width, dtype=F32), struct(1, width, dtype=F32),
        ),
        compiler_params=params(),
    )(gathered, gain_row, router_rows)
    return (
        layer.reshape(micro, sub, width), grad.reshape(micro, sub, width), grad_router.T, grad_gain.reshape(width)
    )


def solution(mesh):
    tokens = P(None, ("section", "expert"), None)
    maps = P("expert", "dp", "section")
    return jax.shard_map(
        functools.partial(shards, mesh.shape["dp"]),
        mesh=mesh,
        in_specs=(tokens, tokens, maps, maps, maps, P(), P(), tokens),
        out_specs=(tokens, tokens, P(), P()),
        check_vma=False,
    )
```
